32 devices in a mesh: ctx: 8 (over z, x), wsh: 4 (over y, core).
Axes of the slice: x: 2, y: 2, z: 4, core: 2. Of those that a mesh axis runs over, the one named last changes fastest.
Arguments:
- block_in: bfloat16 [4, 1024, 1088], P('wsh', 'ctx'), may hold values from -6 to 6
- doc_flags: int32 [4, 1024], P('wsh', 'ctx'), may hold values from 0 to 1, as said below
- ln1_gain: bfloat16 [1088], P('wsh'), may hold values from 0.5 to 1.5
- ln1_bias: bfloat16 [1088], P('wsh'), may hold values from -1 to 1
- w_qkv: bfloat16 [1088, 3264], P('wsh'), may hold values from -0.1875 to 0.1875
- qv_bias: bfloat16 [2176], P('wsh'), may hold values from -1 to 1
- w_out: bfloat16 [1088, 1088], P('wsh'), may hold values from -2 to 2
- out_bias: bfloat16 [1088], P('wsh'), may hold values from -1 to 1
- ln2_gain: bfloat16 [1088], P('wsh'), may hold values from 0.5 to 1.5
- ln2_bias: bfloat16 [1088], P('wsh'), may hold values from -1 to 1
- w_up: bfloat16 [1088, 4352], P(None, 'wsh'), may hold values from -0.1875 to 0.1875
- up_bias: bfloat16 [4352], P('wsh'), may hold values from -1 to 1
- w_down: bfloat16 [4352, 1088], P('wsh'), may hold values from -0.09375 to 0.09375
- down_bias: bfloat16 [1088], P('wsh'), may hold values from -1 to 1
- cotangent: bfloat16 [4, 1024, 1088], P('wsh', 'ctx'), may hold values from -6 to 6
Outputs:
- block_out: bfloat16 [4, 1024, 1088], P('wsh', 'ctx')
- input_grad: bfloat16 [4, 1024, 1088], P('wsh', 'ctx')
- grad_ln1_gain: float32 [1088], P('wsh')
- grad_ln1_bias: float32 [1088], P('wsh')
- grad_w_qkv: float32 [1088, 3264], P('wsh')
- grad_qv_bias: float32 [2176], P('wsh')
- grad_w_out: float32 [1088, 1088], P('wsh')
- grad_out_bias: float32 [1088], P('wsh')
- grad_ln2_gain: float32 [1088], P('wsh')
- grad_ln2_bias: float32 [1088], P('wsh')
- grad_w_up: float32 [1088, 4352], P(None, 'wsh')
- grad_up_bias: float32 [4352], P('wsh')
- grad_w_down: float32 [4352, 1088], P('wsh')
- grad_down_bias: float32 [1088], P('wsh')
- rms_values: float32 [4, 3], P('wsh')
The draws below stay inside these ranges and needn't reach their ends.
Inputs may be any that keep to these rules, and one draw needn't show every extreme that they name: `doc_flags`: each stream has a 1 at position 0. In one stream, one document starts within the first 128 positions and ends within the last 128, and every other document of that stream lies inside those two ranges. In every other stream no document has more than 256 tokens, and one has exactly 256.
All inputs are finite; a program needn't handle non-finite values.
Results may differ from the reference program's by a relative error of at most 0.03.
Values may be sent and summed in bfloat16 or wider, within the bound.
No kernel may reach another device: no remote copies, remote signals or barrier semaphores. Data moves between devices by JAX's collectives and lax.ppermute only.
A program may use at most 448 MiB of HBM per device.

```python
import math
import jax
import jax.numpy as jnp
from jax import lax

D = 1088
H = 17
HD = 64
FF = 4352
TOK_DEV = 128
STREAM_LEN = 1024
STREAMS = 4
DOC_MOST = 256
N_CTX = 8


def draw_doc_flags(key, part):
    key = jax.random.fold_in(key, 11)
    first_key, second_key, third_key, gap_key, force_key, pick_key = jax.random.split(key, 6)
    places = jnp.arange(STREAM_LEN, dtype=jnp.int32)[None, :]
    start_big = jax.random.randint(first_key, (STREAMS, 1), TOK_DEV // 4, 3 * TOK_DEV // 4 + 1)
    end_big = STREAM_LEN - TOK_DEV + jax.random.randint(second_key, (STREAMS, 1), TOK_DEV // 4, 3 * TOK_DEV // 4 + 1)
    coins = jax.random.randint(third_key, (STREAMS, STREAM_LEN), 0, max(TOK_DEV // 16, 2)) == 0
    outside = (places < start_big) | (places > end_big)
    spanning = coins & outside | (places == 0) | (places == start_big) | (places == end_big + 1)
    gaps = jax.random.randint(gap_key, (STREAMS, STREAM_LEN), 1, DOC_MOST + 1)
    forced = jax.random.randint(force_key, (STREAMS, 1), 0, 2)
    gaps = jnp.where(places == forced, DOC_MOST, gaps)
    next_starts = jnp.cumsum(gaps, axis=1).astype(jnp.int32)
    stream_rows = jnp.broadcast_to(jnp.arange(STREAMS, dtype=jnp.int32)[:, None], (STREAMS, STREAM_LEN))
    gapped = jnp.zeros((STREAMS, STREAM_LEN), jnp.int32).at[stream_rows, next_starts].set(1, mode='drop')
    gapped = (gapped == 1) | (places == 0)
    chosen = jax.random.randint(pick_key, (), 0, STREAMS)
    use_span = jnp.arange(STREAMS, dtype=jnp.int32)[:, None] == chosen
    starts = jnp.where(use_span, spanning, gapped)
    return jnp.where(starts, 1, 0).astype(jnp.int32)


def steps_of(rng, extent, shards, least, top_value):
    level = 1.0
    for axis_at, blocks in shards:
        heights = jax.random.uniform(jax.random.fold_in(jax.random.fold_in(rng, 6), axis_at), (blocks,), jnp.float32, least / len(shards), top_value / len(shards))
        level = level * jnp.repeat(jnp.exp(heights), extent[axis_at] // blocks).reshape((-1,) + (1,) * (len(extent) - 1 - axis_at))
    return level


def centred(key, dims, width, most, shards=(), held_as=jnp.bfloat16):
    factor_of = steps_of(key, dims, shards, -0.22, 0.18) if shards else 1.0
    array = jax.random.normal(key, dims, jnp.float32) * width * factor_of
    return jnp.minimum(jnp.maximum(array, -most), most).astype(held_as)


def setup_inputs(seed: int = 0) -> dict:
    arg_keys = jax.random.split(jax.random.key(seed), 16)
    return {
        "block_in": centred(arg_keys[0], (STREAMS, STREAM_LEN, D), 1.0, 6.0, ((0, 4), (1, 8))),
        "doc_flags": draw_doc_flags(jax.random.fold_in(arg_keys[15], 71), 0),
        "ln1_gain": jnp.clip(1.0 + 0.1 * jax.random.normal(arg_keys[2], (D,), jnp.float32), 0.5, 1.5).astype(jnp.bfloat16),
        "ln1_bias": centred(arg_keys[3], (D,), 0.2, 1.0, ((0, 4),)),
        "w_qkv": centred(arg_keys[4], (D, 3 * D), D ** -0.5, 0.1875, ((0, 4),)),
        "qv_bias": centred(arg_keys[5], (2 * D,), 0.2, 1.0, ((0, 4),)),
        "w_out": centred(arg_keys[6], (D, D), (max(D * 8 // (TOK_DEV * N_CTX), 1)) ** -0.5, 2.0, ((0, 4),)),
        "out_bias": centred(arg_keys[7], (D,), 0.2, 1.0, ((0, 4),)),
        "ln2_gain": jnp.clip(1.0 + 0.1 * jax.random.normal(arg_keys[8], (D,), jnp.float32), 0.5, 1.5).astype(jnp.bfloat16),
        "ln2_bias": centred(arg_keys[9], (D,), 0.2, 1.0, ((0, 4),)),
        "w_up": centred(arg_keys[10], (D, FF), D ** -0.5, 0.1875, ((1, 4),)),
        "up_bias": centred(arg_keys[11], (FF,), 0.2, 1.0, ((0, 4),)),
        "w_down": centred(arg_keys[12], (FF, D), FF ** -0.5, 0.09375, ((0, 4),)),
        "down_bias": centred(arg_keys[13], (D,), 0.2, 1.0, ((0, 4),)),
        "cotangent": centred(arg_keys[14], (STREAMS, STREAM_LEN, D), 1.0, 6.0, ((0, 4), (1, 8))),
    }


EPSILON = 1e-05

@jax.custom_vjp
def low(v):
    return lax.optimization_barrier(v.astype(jnp.bfloat16)).astype(jnp.float32)

@jax.custom_vjp
def low_back(v):
    return v

def low_keep(v):
    return (low(v), None)

def low_pass(kept, grad):
    return (grad,)

def back_keep(v):
    return (v, None)

def back_low(kept, grad):
    return (low(grad),)
low.defvjp(low_keep, low_pass)
low_back.defvjp(back_keep, back_low)

def normed(values, gain, shift):
    centre = values - lax.optimization_barrier(jnp.mean(values, axis=-1, keepdims=True))
    spread = lax.optimization_barrier(jnp.mean(centre * centre, axis=-1, keepdims=True))
    return centre * lax.rsqrt(spread + EPSILON) * gain + shift

def attend_stream(queries, key_rows, value_rows, segment, places):
    length = queries.shape[0]
    block_rows = math.gcd(length, 512)
    scaling = HD ** (-0.5)

    def one_block(inputs):
        query_block, segment_block, place_block = inputs
        score_block = jnp.einsum('qhd,khd->qhk', query_block, key_rows, precision=lax.Precision.HIGHEST) * scaling
        score_block = low_back(score_block)
        allowed = ((segment_block[:, None] == segment[None, :]) & (places[None, :] <= place_block[:, None]))[:, None, :]
        probability = jax.nn.softmax(jnp.where(allowed, score_block, -jnp.inf), axis=-1)
        probability = low(probability)
        return jnp.einsum('qhk,khd->qhd', probability, value_rows, precision=lax.Precision.HIGHEST)
    blocks = lax.map(jax.checkpoint(one_block), (queries.reshape(length // block_rows, block_rows, H, HD), segment.reshape(length // block_rows, block_rows), places.reshape(length // block_rows, block_rows)))
    return blocks.reshape(length, H, HD)

def layer_forward(inputs, gain_one, shift_one, w_qkv, qv_bias, w_out, out_bias, gain_two, shift_two, w_up, up_bias, w_down, down_bias, segment, places):
    streams = inputs.shape[0]
    length = inputs.shape[1]
    model_width = inputs.shape[2]
    highest = lax.Precision.HIGHEST
    normed_one = low(normed(inputs, gain_one, shift_one))
    bias_full = jnp.concatenate([qv_bias[:model_width], jnp.zeros((model_width,), qv_bias.dtype), qv_bias[model_width:]])
    projected = low_back(low(jnp.dot(normed_one, w_qkv, precision=highest) + bias_full))
    split_heads = projected.reshape(streams, length, 3, H, HD)

    def per_stream(stream_parts):
        return attend_stream(stream_parts[0], stream_parts[1], stream_parts[2], stream_parts[3], places)
    attended = lax.map(per_stream, (split_heads[:, :, 0], split_heads[:, :, 1], split_heads[:, :, 2], segment))
    attended = low_back(low(attended.reshape(streams, length, model_width)))
    attn_branch = low_back(jnp.dot(attended, w_out, precision=highest) + out_bias)
    residual = inputs + attn_branch
    normed_two = low(normed(residual, gain_two, shift_two))
    hidden_pre = low_back(jnp.dot(normed_two, w_up, precision=highest) + up_bias)
    hidden_act = low(jax.nn.gelu(hidden_pre, approximate=True))
    mlp_branch = low_back(jnp.dot(hidden_act, w_down, precision=highest) + down_bias)
    return (residual + mlp_branch, (attn_branch, mlp_branch))

def reference(block_in, doc_flags, ln1_gain, ln1_bias, w_qkv, qv_bias, w_out, out_bias, ln2_gain, ln2_bias, w_up, up_bias, w_down, down_bias, cotangent):
    segment = (jnp.cumsum(doc_flags, axis=1) - 1).astype(jnp.int32)
    places = jnp.arange(doc_flags.shape[1], dtype=jnp.int32)

    def forward(inputs, gain_one, shift_one, qkv_weight, qv_shift, out_weight, out_shift, gain_two, shift_two, up_weight, up_shift, down_weight, down_shift):
        return layer_forward(inputs, gain_one, shift_one, qkv_weight, qv_shift, out_weight, out_shift, gain_two, shift_two, up_weight, up_shift, down_weight, down_shift, segment, places)
    block_out, pullback, branches = jax.vjp(forward, block_in.astype(jnp.float32), ln1_gain.astype(jnp.float32), ln1_bias.astype(jnp.float32), w_qkv.astype(jnp.float32), qv_bias.astype(jnp.float32), w_out.astype(jnp.float32), out_bias.astype(jnp.float32), ln2_gain.astype(jnp.float32), ln2_bias.astype(jnp.float32), w_up.astype(jnp.float32), up_bias.astype(jnp.float32), w_down.astype(jnp.float32), down_bias.astype(jnp.float32), has_aux=True)
    gradients = pullback(cotangent.astype(jnp.float32))
    attn_branch, mlp_branch = branches
    rms_values = jnp.stack([jnp.sqrt(lax.optimization_barrier(jnp.mean(attn_branch * attn_branch, axis=(1, 2)))), jnp.sqrt(lax.optimization_barrier(jnp.mean(mlp_branch * mlp_branch, axis=(1, 2)))), jnp.sqrt(lax.optimization_barrier(jnp.mean(block_out * block_out, axis=(1, 2))))], axis=1)
    return (block_out.astype(jnp.bfloat16), gradients[0].astype(jnp.bfloat16), gradients[1], gradients[2], gradients[3], gradients[4], gradients[5], gradients[6], gradients[7], gradients[8], gradients[9], gradients[10], gradients[11], gradients[12], rms_values)
```

```python
import functools
import math

import jax
import jax.numpy as jnp
from jax import lax
from jax.experimental import pallas as pl
from jax.experimental.pallas import tpu as pltpu
from jax.sharding import PartitionSpec as P

H = 17
HD = 64
LANES = 128
EPSILON = 1e-05
NEGATIVE = -1e30
LOG2E = math.log2(math.e)
SCORE_SCALE = HD ** (-0.5) * LOG2E
VMEM_MOST = 56 * 2**20

F32 = jnp.float32
BF16 = jnp.bfloat16


def dot_nn(left, right):
    return lax.dot_general(left, right, (((1,), (0,)), ((), ())), preferred_element_type=F32)


def dot_nt(left, right):
    return lax.dot_general(left, right, (((1,), (1,)), ((), ())), preferred_element_type=F32)


def dot_tn(left, right):
    return lax.dot_general(left, right, (((0,), (0,)), ((), ())), preferred_element_type=F32)


def swap(value, axis, distance):
    size = lax.axis_size(axis)
    return lax.ppermute(value, axis, [(i, i ^ distance) for i in range(size)])


def centred(values):
    centre = values - jnp.mean(values, axis=-1, keepdims=True)
    spread = jnp.mean(centre * centre, axis=-1, keepdims=True)
    return centre, lax.rsqrt(spread + EPSILON)


def norm_back(unit, inverse, scaled_grad):
    mean_grad = jnp.mean(scaled_grad, axis=-1, keepdims=True)
    mean_both = jnp.mean(scaled_grad * unit, axis=-1, keepdims=True)
    return inverse * (scaled_grad - mean_grad - unit * mean_both)


QB = 256


def head_lanes(head):
    lane = lax.broadcasted_iota(jnp.int32, (1, LANES), 1)
    return (lane >= HD * head) & (lane < HD * (head + 1))


def masked_scores(keys, queries, start_row, key_at, query_at):
    scores = dot_nt(keys, queries) * SCORE_SCALE
    shape = scores.shape
    key_place = lax.broadcasted_iota(jnp.int32, shape, 0) + key_at
    allowed = key_place >= start_row
    if key_at + shape[0] > query_at:
        query_place = lax.broadcasted_iota(jnp.int32, shape, 1) + query_at
        allowed = allowed & (key_place <= query_place)
    return jnp.where(allowed, scores, NEGATIVE)


def fold_rows(values, combine):
    return combine(values.reshape(values.shape[0] // 8, 8, values.shape[1]), axis=0)


def attend_forward_kernel(
    n_ctx, n_wsh, place_ref, start_ref, gain_ref, shift_ref, bias_ref, *refs
):
    blocks, refs = refs[:n_ctx], refs[n_ctx:]
    weights, refs = refs[:n_wsh], refs[n_wsh:]
    normed_ref, qkv_ref, attended_ref, total_ref, own_ref, *refs = refs
    sends, (weight_ref, score_ref, prob_ref, value_ref) = refs[:n_ctx], refs[n_ctx:]
    ctx, wsh = place_ref[0], place_ref[1]
    tok_rows = blocks[0].shape[0]
    length = n_ctx * tok_rows
    weight_rows = weights[0].shape[0]
    for k in range(n_wsh):
        at = pl.multiple_of((wsh ^ k) * weight_rows, 16)
        weight_ref[pl.ds(at, weight_rows), :] = weights[k][...]
    for j in range(n_ctx):
        at = pl.multiple_of((ctx ^ j) * tok_rows, tok_rows)
        centre, inverse = centred(blocks[j][...].astype(F32))
        values = centre * inverse * gain_ref[...] + shift_ref[...]
        normed_ref[pl.ds(at, tok_rows), :] = values.astype(BF16)
    for at in range(0, length, QB):
        rows = pl.ds(at, QB)
        values = dot_nn(normed_ref[rows, :], weight_ref[...]) + bias_ref[...]
        qkv_ref[rows, :] = values.astype(BF16)
    for group in range(2):
        value_ref[group] = qkv_ref[:, pl.ds((4 + group) * LANES, LANES)].T
    for head in range(3):
        group, half = head // 2, head % 2
        for query_at in range(0, length, QB):
            columns = pl.ds(query_at, QB)
            queries = qkv_ref[columns, pl.ds(group * LANES, LANES)]
            queries = jnp.where(head_lanes(half), queries, 0)
            start_row = start_ref[:, columns]
            best = None
            for key_at in range(0, query_at + QB, QB):
                keys = qkv_ref[pl.ds(key_at, QB), pl.ds((2 + group) * LANES, LANES)]
                scores = masked_scores(keys, queries, start_row, key_at, query_at)
                score_ref[pl.ds(key_at, QB), :] = scores
                most = fold_rows(scores, jnp.max)
                best = most if best is None else jnp.maximum(best, most)
            best = jnp.max(best, axis=0, keepdims=True)
            total = None
            for key_at in range(0, query_at + QB, QB):
                weight = jnp.exp2(score_ref[pl.ds(key_at, QB), :] - best)
                some = fold_rows(weight, jnp.sum)
                total = some if total is None else total + some
                prob_ref[pl.ds(key_at, QB), :] = weight.astype(BF16)
            total = jnp.sum(total, axis=0, keepdims=True)
            reach = query_at + QB
            values = value_ref[group, pl.ds(half * HD, HD), pl.ds(0, reach)]
            weighted = dot_nn(values, prob_ref[pl.ds(0, reach), :])
            attended_ref[pl.ds(head * HD, HD), columns] = weighted / total
            total_ref[pl.ds(head, 1), columns] = best + jnp.log2(total)
    for j in range(n_ctx):
        at = pl.multiple_of((ctx ^ j) * tok_rows, tok_rows)
        sends[j][...] = attended_ref[pl.ds(0, 2 * HD), pl.ds(at, tok_rows)].T.astype(BF16)
    at = pl.multiple_of(ctx * tok_rows, tok_rows)
    shared = attended_ref[pl.ds(2 * HD, HD), pl.ds(at, tok_rows)]
    shared = jnp.concatenate([shared, jnp.zeros_like(shared)], axis=0)
    own_ref[...] = shared.T.astype(BF16)


def attend_forward(place, start_row, gain, shift, bias, blocks, weights):
    n_ctx, n_wsh = len(blocks), len(weights)
    tok_rows, width = blocks[0].shape
    length = n_ctx * tok_rows
    columns = weights[0].shape[1]
    shapes = [
        jax.ShapeDtypeStruct((length, width), BF16),
        jax.ShapeDtypeStruct((length, columns), BF16),
        jax.ShapeDtypeStruct((3 * HD, length), F32),
        jax.ShapeDtypeStruct((8, length), F32),
        jax.ShapeDtypeStruct((tok_rows, LANES), BF16),
    ] + [jax.ShapeDtypeStruct((tok_rows, LANES), BF16)] * n_ctx
    pairs = 3 * length * length // 2
    out = pl.pallas_call(
        functools.partial(attend_forward_kernel, n_ctx, n_wsh),
        out_shape=shapes,
        in_specs=[pl.BlockSpec(memory_space=pltpu.SMEM)]
        + [pl.BlockSpec(memory_space=pltpu.VMEM)] * (4 + n_ctx + n_wsh),
        out_specs=[pl.BlockSpec(memory_space=pltpu.VMEM)] * len(shapes),
        scratch_shapes=[
            pltpu.VMEM((width, columns), BF16),
            pltpu.VMEM((length, QB), F32),
            pltpu.VMEM((length, QB), BF16),
            pltpu.VMEM((2, LANES, length), BF16),
        ],
        compiler_params=pltpu.CompilerParams(vmem_limit_bytes=VMEM_MOST),
        cost_estimate=pl.CostEstimate(
            flops=2 * length * width * columns + 4 * pairs * LANES,
            bytes_accessed=2 * length * (2 * width + columns) + 2 * width * columns,
            transcendentals=pairs,
        ),
        name="attend_forward",
    )(place, start_row, gain, shift, bias, *blocks, *weights)
    normed, qkv, attended, total, own, *sends = out
    return normed, qkv, attended, total, own, sends


def attend_backward_kernel(n_ctx, place_ref, start_ref, qkv_ref, attended_ref, total_ref, *refs):
    grads, (all_ref, own_ref, *refs) = refs[:n_ctx], refs[n_ctx:]
    sends, (grad_ref, key_ref, turned_ref, sum_ref, query_ref) = refs[:n_ctx], refs[n_ctx:]
    ctx = place_ref[0]
    tok_rows = grads[0].shape[0]
    length = n_ctx * tok_rows
    for j in range(n_ctx):
        at = pl.multiple_of((ctx ^ j) * tok_rows, tok_rows)
        grad_ref[pl.ds(at, tok_rows), :] = grads[j][...]
    for group in range(2):
        key_ref[group] = qkv_ref[:, pl.ds((2 + group) * LANES, LANES)].T
        turned_ref[group] = grad_ref[:, pl.ds(group * LANES, LANES)].T
    sum_ref[...] = jnp.zeros_like(sum_ref)
    for head in range(3):
        group, half = head // 2, head % 2
        for query_at in range(0, length, QB):
            columns = pl.ds(query_at, QB)
            lanes = head_lanes(half)
            queries = qkv_ref[columns, pl.ds(group * LANES, LANES)]
            queries = jnp.where(lanes, queries, 0)
            grad = jnp.where(lanes, grad_ref[columns, pl.ds(group * LANES, LANES)], 0)
            start_row = start_ref[:, columns]
            total = total_ref[pl.ds(head, 1), columns]
            turned = turned_ref[group, pl.ds(half * HD, HD), columns].astype(F32)
            delta = turned * attended_ref[pl.ds(head * HD, HD), columns]
            delta = jnp.sum(delta, axis=0, keepdims=True)
            query_grad = None
            for key_at in range(0, query_at + QB, QB):
                rows = pl.ds(key_at, QB)
                keys = qkv_ref[rows, pl.ds((2 + group) * LANES, LANES)]
                values = qkv_ref[rows, pl.ds((4 + group) * LANES, LANES)]
                scores = masked_scores(keys, queries, start_row, key_at, query_at)
                prob = jnp.exp2(scores - total)
                score_grad = (prob * (dot_nt(values, grad) - delta)).astype(BF16)
                sum_ref[1, rows, pl.ds(group * LANES, LANES)] += dot_nn(prob.astype(BF16), grad)
                sum_ref[0, rows, pl.ds(group * LANES, LANES)] += dot_nn(score_grad, queries)
                part = dot_nn(key_ref[group, pl.ds(half * HD, HD), rows], score_grad)
                query_grad = part if query_grad is None else query_grad + part
            query_ref[pl.ds(head * HD, HD), columns] = query_grad * HD ** (-0.5)
    query_ref[pl.ds(3 * HD, HD), :] = jnp.zeros((HD, length), F32)
    for group in range(2):
        lanes = pl.ds(group * LANES, LANES)
        all_ref[:, lanes] = query_ref[pl.ds(group * LANES, LANES), :].T.astype(BF16)
        key_grad = sum_ref[0, :, lanes] * HD ** (-0.5)
        all_ref[:, pl.ds((2 + group) * LANES, LANES)] = key_grad.astype(BF16)
        all_ref[:, pl.ds((4 + group) * LANES, LANES)] = sum_ref[1, :, lanes].astype(BF16)
    for part in range(3):
        lanes = pl.ds(part * LANES, LANES)
        for j in range(n_ctx):
            at = pl.multiple_of((ctx ^ j) * tok_rows, tok_rows)
            sends[j][:, lanes] = all_ref[pl.ds(at, tok_rows), pl.ds(2 * part * LANES, LANES)]
        at = pl.multiple_of(ctx * tok_rows, tok_rows)
        own_ref[:, lanes] = all_ref[pl.ds(at, tok_rows), pl.ds((2 * part + 1) * LANES, LANES)]


def attend_backward(place, start_row, qkv, attended, total, grads):
    n_ctx = len(grads)
    tok_rows = grads[0].shape[0]
    length = n_ctx * tok_rows
    shapes = [
        jax.ShapeDtypeStruct((length, 6 * LANES), BF16),
        jax.ShapeDtypeStruct((tok_rows, 3 * LANES), BF16),
    ] + [jax.ShapeDtypeStruct((tok_rows, 3 * LANES), BF16)] * n_ctx
    pairs = 3 * length * length // 2
    every, own, *sends = pl.pallas_call(
        functools.partial(attend_backward_kernel, n_ctx),
        out_shape=shapes,
        in_specs=[pl.BlockSpec(memory_space=pltpu.SMEM)]
        + [pl.BlockSpec(memory_space=pltpu.VMEM)] * (4 + n_ctx),
        out_specs=[pl.BlockSpec(memory_space=pltpu.VMEM)] * len(shapes),
        scratch_shapes=[
            pltpu.VMEM((length, 2 * LANES), BF16),
            pltpu.VMEM((2, LANES, length), BF16),
            pltpu.VMEM((2, LANES, length), BF16),
            pltpu.VMEM((2, length, 2 * LANES), F32),
            pltpu.VMEM((2 * LANES, length), F32),
        ],
        compiler_params=pltpu.CompilerParams(vmem_limit_bytes=VMEM_MOST),
        cost_estimate=pl.CostEstimate(
            flops=10 * pairs * LANES,
            bytes_accessed=2 * length * 20 * LANES,
            transcendentals=pairs,
        ),
        name="attend_backward",
    )(place, start_row, qkv, attended, total, *grads)
    return every, own, sends


def out_project_kernel(
    n_ctx, n_wsh, place_ref, own_ref, in_ref, bias_ref, gain_ref, shift_ref, *refs
):
    parts, refs = refs[:n_ctx], refs[n_ctx:]
    weights, refs = refs[:n_wsh], refs[n_wsh:]
    low_ref, residual_ref, normed_ref, square_ref, weight_ref = refs
    ctx, wsh = place_ref[0], place_ref[1]
    weight_rows = weights[0].shape[0]
    for k in range(n_wsh):
        at = pl.multiple_of((wsh ^ k) * weight_rows, 16)
        weight_ref[pl.ds(at, weight_rows), :] = weights[k][...]
    for j in range(n_ctx):
        at = pl.multiple_of((ctx ^ j) * LANES, LANES)
        low_ref[:, pl.ds(at, LANES)] = parts[j][...]
    low_ref[:, pl.ds(n_ctx * LANES, HD)] = own_ref[:, pl.ds(0, HD)]
    branch = dot_nn(low_ref[...], weight_ref[...]) + bias_ref[...]
    square_ref[...] = jnp.sum(branch * branch, axis=0, keepdims=True)
    residual = in_ref[...].astype(F32) + branch
    residual_ref[...] = residual
    centre, inverse = centred(residual)
    normed_ref[...] = (centre * inverse * gain_ref[...] + shift_ref[...]).astype(BF16)


def whole_call(kernel, name, shapes, scratch, flops, place, *arrays):
    moved = sum(a.size * a.dtype.itemsize for a in arrays)
    moved += sum(math.prod(s.shape) * s.dtype.itemsize for s in shapes)
    return pl.pallas_call(
        kernel,
        out_shape=shapes,
        in_specs=[pl.BlockSpec(memory_space=pltpu.SMEM)]
        + [pl.BlockSpec(memory_space=pltpu.VMEM)] * len(arrays),
        out_specs=[pl.BlockSpec(memory_space=pltpu.VMEM)] * len(shapes),
        scratch_shapes=scratch,
        compiler_params=pltpu.CompilerParams(vmem_limit_bytes=VMEM_MOST),
        cost_estimate=pl.CostEstimate(flops=flops, bytes_accessed=moved, transcendentals=0),
        name=name,
    )(place, *arrays)


def out_project(place, own, rows_in, bias, gain, shift, parts, weights):
    tok_rows, width = rows_in.shape
    return whole_call(
        functools.partial(out_project_kernel, len(parts), len(weights)),
        "out_project",
        [
            jax.ShapeDtypeStruct((tok_rows, width), BF16),
            jax.ShapeDtypeStruct((tok_rows, width), F32),
            jax.ShapeDtypeStruct((tok_rows, width), BF16),
            jax.ShapeDtypeStruct((1, width), F32),
        ],
        [pltpu.VMEM((width, width), BF16)],
        2 * tok_rows * width * width,
        place,
        own,
        rows_in,
        bias,
        gain,
        shift,
        *parts,
        *weights,
    )


GELU_SLOPE = math.sqrt(2 / math.pi)
GELU_CUBE = 0.044715


def feed_kernel(
    first_ref,
    second_ref,
    first_grad_ref,
    second_grad_ref,
    up_ref,
    bias_ref,
    down_ref,
    act_ref,
    pre_ref,
    first_back_ref,
    second_back_ref,
    first_out_ref,
    second_out_ref,
    shift_ref,
):
    tok_rows = first_ref.shape[0]
    sums = 0.0
    for at, rows_ref, grads_ref, back_ref, out_ref in (
        (0, first_ref, first_grad_ref, first_back_ref, first_out_ref),
        (tok_rows, second_ref, second_grad_ref, second_back_ref, second_out_ref),
    ):
        rows = pl.ds(at, tok_rows)
        hidden = dot_nn(rows_ref[...], up_ref[...]) + bias_ref[...]
        square = hidden * hidden
        turn = jnp.tanh(hidden * (GELU_SLOPE + GELU_SLOPE * GELU_CUBE * square))
        half = 0.5 + 0.5 * turn
        act = (hidden * half).astype(BF16)
        act_ref[rows, :] = act
        slope = half + 0.5 * hidden * (1.0 - turn * turn) * (
            GELU_SLOPE + 3 * GELU_SLOPE * GELU_CUBE * square
        )
        pre = (dot_nt(grads_ref[...], down_ref[...]) * slope).astype(BF16)
        pre_ref[rows, :] = pre
        sums = sums + jnp.sum(pre.astype(F32), axis=0, keepdims=True)
        back_ref[...] = dot_nt(pre, up_ref[...]).astype(back_ref.dtype)
        out_ref[...] = dot_nn(act, down_ref[...]).astype(out_ref.dtype)
    shift_ref[...] = sums


def feed_forward(place, first, second, first_grad, second_grad, up, bias, down, first_type, name):
    tok_rows, width = first.shape
    units = up.shape[1]

    def kernel(place_ref, *refs):
        feed_kernel(*refs)

    return whole_call(
        kernel,
        name,
        [
            jax.ShapeDtypeStruct((2 * tok_rows, units), BF16),
            jax.ShapeDtypeStruct((2 * tok_rows, units), BF16),
            jax.ShapeDtypeStruct((tok_rows, width), first_type),
            jax.ShapeDtypeStruct((tok_rows, width), BF16),
            jax.ShapeDtypeStruct((tok_rows, width), first_type),
            jax.ShapeDtypeStruct((tok_rows, width), BF16),
            jax.ShapeDtypeStruct((1, units), F32),
        ],
        [],
        16 * tok_rows * width * units,
        place,
        first,
        second,
        first_grad,
        second_grad,
        up,
        bias,
        down,
    )


def residual_back_kernel(
    n_ctx, n_wsh, place_ref, own_ref, near_ref, far_ref, residual_ref, cotangent_ref, gain_ref, *refs
):
    weights, refs = refs[:n_wsh], refs[n_wsh:]
    total_ref, low_ref, sum_gain_ref, sum_shift_ref, sum_low_ref, *refs = refs
    sends, (weight_ref,) = refs[:n_ctx], refs[n_ctx:]
    ctx, wsh = place_ref[0], place_ref[1]
    weight_rows = weights[0].shape[0]
    for k in range(n_wsh):
        at = pl.multiple_of((wsh ^ k) * weight_rows, 16)
        weight_ref[pl.ds(at, weight_rows), :] = weights[k][...]
    grad = own_ref[...] + near_ref[...].astype(F32) + far_ref[...].astype(F32)
    centre, inverse = centred(residual_ref[...])
    unit = centre * inverse
    sum_gain_ref[...] = jnp.sum(grad * unit, axis=0, keepdims=True)
    sum_shift_ref[...] = jnp.sum(grad, axis=0, keepdims=True)
    total = cotangent_ref[...].astype(F32) + norm_back(unit, inverse, grad * gain_ref[...])
    total_ref[...] = total
    low = total.astype(BF16)
    low_ref[...] = low
    sum_low_ref[...] = jnp.sum(low.astype(F32), axis=0, keepdims=True)
    shared = dot_nt(low, weight_ref[pl.ds(n_ctx * LANES, HD), :])
    shared = jnp.concatenate([shared, jnp.zeros_like(shared)], axis=1).astype(BF16)
    for j in range(n_ctx):
        at = pl.multiple_of((ctx ^ j) * LANES, LANES)
        sends[j][:, pl.ds(0, LANES)] = dot_nt(low, weight_ref[pl.ds(at, LANES), :]).astype(BF16)
        sends[j][:, pl.ds(LANES, LANES)] = shared


def residual_back(place, own, near, far, residual, cotangent, gain, weights, n_ctx):
    tok_rows, width = residual.shape
    row = jax.ShapeDtypeStruct((1, width), F32)
    out = whole_call(
        functools.partial(residual_back_kernel, n_ctx, len(weights)),
        "residual_back",
        [
            jax.ShapeDtypeStruct((tok_rows, width), F32),
            jax.ShapeDtypeStruct((tok_rows, width), BF16),
            row,
            row,
            row,
        ]
        + [jax.ShapeDtypeStruct((tok_rows, 2 * LANES), BF16)] * n_ctx,
        [pltpu.VMEM((width, width), BF16)],
        2 * tok_rows * width * width,
        place,
        own,
        near,
        far,
        residual,
        cotangent,
        gain,
        *weights,
    )
    total, low, sum_gain, sum_shift, sum_low, *sends = out
    return total, low, sum_gain, sum_shift, sum_low, sends


def input_back_kernel(n_ctx, n_wsh, place_ref, own_ref, in_ref, total_ref, gain_ref, *refs):
    parts, refs = refs[:n_ctx], refs[n_ctx:]
    weights, refs = refs[:n_wsh], refs[n_wsh:]
    back_ref, sum_gain_ref, sum_shift_ref, weight_ref, grad_ref = refs
    ctx, wsh = place_ref[0], place_ref[1]
    weight_rows = weights[0].shape[0] // 3
    grad = 0.0
    for part in range(3):
        for k in range(n_wsh):
            at = pl.multiple_of((wsh ^ k) * weight_rows, 16)
            rows = pl.ds(part * weight_rows, weight_rows)
            weight_ref[pl.ds(at, weight_rows), :] = weights[k][rows, :]
        for j in range(n_ctx):
            at = pl.multiple_of((ctx ^ j) * LANES, LANES)
            grad_ref[:, pl.ds(at, LANES)] = parts[j][:, pl.ds(part * LANES, LANES)]
        grad_ref[:, pl.ds(n_ctx * LANES, HD)] = own_ref[:, pl.ds(part * LANES, HD)]
        grad = grad + dot_nt(grad_ref[...], weight_ref[...])
    centre, inverse = centred(in_ref[...].astype(F32))
    unit = centre * inverse
    sum_gain_ref[...] = jnp.sum(grad * unit, axis=0, keepdims=True)
    sum_shift_ref[...] = jnp.sum(grad, axis=0, keepdims=True)
    total = total_ref[...] + norm_back(unit, inverse, grad * gain_ref[...])
    back_ref[...] = total.astype(BF16)


def input_back(place, own, rows_in, total, gain, parts, weights):
    tok_rows, width = rows_in.shape
    row = jax.ShapeDtypeStruct((1, width), F32)
    return whole_call(
        functools.partial(input_back_kernel, len(parts), len(weights)),
        "input_back",
        [jax.ShapeDtypeStruct((tok_rows, width), BF16), row, row],
        [pltpu.VMEM((width, width), BF16), pltpu.VMEM((tok_rows, width), BF16)],
        6 * tok_rows * width * width,
        place,
        own,
        rows_in,
        total,
        gain,
        *parts,
        *weights,
    )


def lay_rows_kernel(place_ref, *refs):
    *parts, out_ref = refs
    rows = parts[0].shape[0]
    for j, part in enumerate(parts):
        at = pl.multiple_of((place_ref[0] ^ j) * rows, 8)
        out_ref[pl.ds(at, rows), :] = part[...].astype(F32)


def lay_rows(place, parts):
    rows, columns = parts[0].shape
    shape = jax.ShapeDtypeStruct((rows * len(parts), columns), F32)
    return whole_call(lay_rows_kernel, "lay_rows", [shape], [], 0, place, *parts)[0]


def lay_qkv_kernel(place_ref, own_ref, *refs):
    *parts, out_ref, row_ref = refs
    n_ctx = len(parts)
    width = row_ref.shape[1]
    for kind in range(3):
        for j, part in enumerate(parts):
            at = pl.multiple_of((place_ref[0] ^ j) * LANES, LANES)
            row_ref[:, pl.ds(at, LANES)] = part[:, pl.ds(kind * LANES, LANES)].astype(F32)
        shared = own_ref[:, pl.ds(kind * LANES, LANES)].astype(F32)
        row_ref[:, pl.ds(n_ctx * LANES, HD)] = shared[:, :HD]
        out_ref[:, pl.ds(kind * width, width)] = row_ref[...]


def lay_qkv(place, own, parts, width):
    rows = own.shape[0]
    shape = jax.ShapeDtypeStruct((rows, 3 * width), F32)
    scratch = [pltpu.VMEM((rows, width), F32)]
    return whole_call(lay_qkv_kernel, "lay_qkv", [shape], scratch, 0, place, own, *parts)[0]


def gather_wsh(block):
    across = swap(block, "wsh", 2)
    return [block, swap(block, "wsh", 1), across, swap(across, "wsh", 1)]


def gather_ctx(block):
    far = [block] + [swap(block, "ctx", j) for j in (2, 4, 6)]
    near = [swap(part, "ctx", 1) for part in far]
    return [part for pair in zip(far, near) for part in pair]


def ordered(parts, mine):
    return [
        sum(jnp.where(mine ^ k == i, part, jnp.zeros_like(part)) for k, part in enumerate(parts))
        for i in range(len(parts))
    ]


def pick(pieces, index, axis=0):
    return lax.dynamic_index_in_dim(pieces, index, axis, keepdims=False)


def scatter_ctx(grad, ctx):
    rows, columns = grad.shape
    near, far = ctx & 1, ctx >> 1
    pieces = grad.reshape(4, 2, rows // 8, columns)
    kept = pick(pieces, near, 1)
    half = kept + swap(pick(pieces, 1 - near, 1).astype(BF16), "ctx", 1).astype(F32)
    total = pick(half, far)
    for k in range(1, 4):
        total = total + swap(pick(half, far ^ k).astype(BF16), "ctx", 2 * k).astype(F32)
    return total.astype(BF16)


def sum_over(value, axis):
    distance = 1
    while distance < lax.axis_size(axis):
        value = value + swap(value, axis, distance)
        distance *= 2
    return value


def by_heads(
    block_in,
    doc_flags,
    ln1_gain,
    ln1_bias,
    w_qkv,
    qv_bias,
    w_out,
    out_bias,
    ln2_gain,
    ln2_bias,
    w_up,
    up_bias,
    w_down,
    down_bias,
    cotangent,
):
    n_ctx, n_wsh = lax.axis_size("ctx"), lax.axis_size("wsh")
    ctx, wsh = lax.axis_index("ctx"), lax.axis_index("wsh")
    place = jnp.stack([ctx, wsh]).astype(jnp.int32)
    tok_rows, width = block_in.shape[1:]
    length = n_ctx * tok_rows
    shard = ln1_gain.shape[0]
    rows_in, rows_grad = block_in[0], cotangent[0]

    blocks = gather_ctx(rows_in)
    columns = []
    for kind in range(3):
        pair = lax.dynamic_slice_in_dim(w_qkv, kind * width + ctx * LANES, LANES, 1)
        shared = w_qkv[:, (kind + 1) * width - HD : (kind + 1) * width]
        columns += [pair, shared, jnp.zeros((shard, LANES - HD), BF16)]
    weight_parts = gather_wsh(jnp.concatenate(columns, axis=1))

    packed = jnp.concatenate([ln1_gain, ln1_bias, qv_bias, out_bias, ln2_gain, ln2_bias, down_bias])
    packed = jnp.stack(ordered(gather_wsh(packed), wsh)).astype(F32)

    def vector(at, size):
        return packed[:, at * shard : at * shard + size].reshape(1, n_wsh * size)

    gain_one, shift_one, qv_full = vector(0, shard), vector(1, shard), vector(2, 2 * shard)
    out_shift, gain_two, shift_two, down_shift = [vector(at, shard) for at in (4, 5, 6, 7)]
    gap = jnp.zeros((1, LANES - HD), F32)
    query_shift = lax.dynamic_slice_in_dim(qv_full, ctx * LANES, LANES, 1)
    value_shift = lax.dynamic_slice_in_dim(qv_full, width + ctx * LANES, LANES, 1)
    head_shift = jnp.concatenate(
        [
            query_shift,
            qv_full[:, width - HD : width],
            gap,
            jnp.zeros((1, 2 * LANES), F32),
            value_shift,
            qv_full[:, 2 * width - HD :],
            gap,
        ],
        axis=1,
    )

    flags = doc_flags
    for distance in (1, 2, 4):
        flags = jnp.concatenate([flags, swap(flags, "ctx", distance)], axis=0)
    flags = jnp.concatenate(ordered([flags[j : j + 1] for j in range(n_ctx)], ctx), axis=1)
    places = jnp.arange(length, dtype=jnp.int32)
    started = jnp.where(flags[0] == 1, places, 0)
    start_row = jnp.max(
        jnp.where(places[:, None] <= places[None, :], started[:, None], 0), axis=0, keepdims=True
    )

    out_parts = gather_wsh(w_out)
    grads = gather_wsh(rows_grad)
    qkv_rows = jnp.concatenate([w_qkv[:, k * width : (k + 1) * width] for k in range(3)], axis=0)

    normed_one, qkv, attended, log_total, own_low, sends = attend_forward(
        place, start_row, gain_one, shift_one, head_shift, blocks, weight_parts
    )
    parts = [sends[0]] + [swap(sends[j], "ctx", j) for j in range(1, n_ctx)]
    attended_low, residual, normed_two, branch_squares = out_project(
        place, own_low, rows_in, out_shift, gain_two, shift_two, parts, out_parts
    )
    normed_parts = gather_wsh(normed_two)
    unit_shift = up_bias.astype(F32).reshape(1, -1)
    act_near, pre_near, back_0, back_1, out_0, out_1, up_sum_near = feed_forward(
        place,
        normed_parts[0],
        normed_parts[1],
        grads[0],
        grads[1],
        w_up,
        unit_shift,
        w_down,
        F32,
        "feed_near",
    )
    act_far, pre_far, back_2, back_3, out_2, out_3, up_sum_far = feed_forward(
        place,
        normed_parts[2],
        normed_parts[3],
        grads[2],
        grads[3],
        w_up,
        unit_shift,
        w_down,
        F32,
        "feed_far",
    )

    def to_streams(part_1, part_2, part_3):
        near = swap(part_1, "wsh", 1)
        across = part_2 + swap(part_3, "wsh", 1).astype(F32)
        return near, swap(across.astype(BF16), "wsh", 2)

    back_near, back_across = to_streams(back_1, back_2, back_3)
    residual_grad, attn_grad, sum_gain_two, sum_shift_two, sum_attn, grad_sends = residual_back(
        place, back_0, back_near, back_across, residual, rows_grad, gain_two, out_parts, n_ctx
    )
    grad_parts = [grad_sends[0]] + [swap(grad_sends[j], "ctx", j) for j in range(1, n_ctx)]
    qkv_grad, own_grad, qkv_sends = attend_backward(
        place, start_row, qkv, attended, log_total, grad_parts
    )
    qkv_parts = [qkv_sends[0]] + [swap(qkv_sends[j], "ctx", j) for j in range(1, n_ctx)]
    weight_full = gather_wsh(qkv_rows)
    input_grad, sum_gain_one, sum_shift_one = input_back(
        place, own_grad, rows_in, residual_grad, gain_one, qkv_parts, weight_full
    )

    out_near, out_across = to_streams(out_1, out_2, out_3)
    mlp_branch = out_0 + out_near.astype(F32) + out_across.astype(F32) + down_shift
    block_full = residual + mlp_branch
    squares = jnp.stack(
        [jnp.sum(branch_squares), jnp.sum(mlp_branch * mlp_branch), jnp.sum(block_full * block_full)]
    )

    act = jnp.concatenate([act_near, act_far], axis=0)
    pre = jnp.concatenate([pre_near, pre_far], axis=0)
    rows_two = jnp.concatenate(normed_parts, axis=0)
    all_grads = jnp.concatenate(grads, axis=0)
    grad_down = lay_rows(place, gather_ctx(scatter_ctx(dot_tn(act, all_grads), ctx)))
    grad_up = lay_rows(place, gather_ctx(scatter_ctx(dot_tn(rows_two, pre), ctx)))

    def scatter_wsh(grad):
        pieces = grad.reshape(n_wsh, grad.shape[0] // n_wsh, grad.shape[1])
        part = [pick(pieces, wsh ^ k) for k in range(n_wsh)]
        near, across = to_streams(part[1].astype(BF16), part[2], part[3].astype(BF16))
        return part[0] + near.astype(F32) + across.astype(F32)

    out_piece = scatter_wsh(dot_tn(attended_low, attn_grad))
    out_piece = jnp.pad(out_piece, ((0, 112), (0, 0)))
    grad_out = lay_rows(place, gather_ctx(scatter_ctx(out_piece, ctx)))[:shard]
    head_grad = scatter_wsh(dot_tn(normed_one, qkv_grad)).astype(BF16)
    pair_grad = jnp.concatenate([head_grad[:, 2 * k * LANES : (2 * k + 1) * LANES] for k in range(3)], 1)
    own_piece = jnp.concatenate(
        [head_grad[:, (2 * k + 1) * LANES : (2 * k + 2) * LANES] for k in range(3)], 1
    )
    grad_qkv = lay_qkv(place, own_piece, gather_ctx(pair_grad), width)

    head_sums = jnp.sum(qkv_grad.astype(F32), axis=0, keepdims=True)
    first = jnp.where(ctx == 0, 1.0, 0.0)
    qv_sum = jnp.zeros((1, 2 * width), F32)
    for kind, at in ((0, 0), (2, width)):
        pair = head_sums[:, 2 * kind * LANES : (2 * kind + 1) * LANES]
        shared = head_sums[:, (2 * kind + 1) * LANES : (2 * kind + 1) * LANES + HD]
        qv_sum = lax.dynamic_update_slice(qv_sum, pair, (0, at + ctx * LANES))
        qv_sum = lax.dynamic_update_slice(qv_sum, shared * first, (0, at + n_ctx * LANES))
    sum_down = jnp.sum(rows_grad.astype(F32), axis=0, keepdims=True)
    early = jnp.concatenate([sum_gain_two, sum_shift_two, sum_attn, sum_down], axis=1)
    along = jnp.concatenate([early, up_sum_near + up_sum_far, squares.reshape(1, 3)], axis=1)
    along = sum_over(along, "ctx")
    early = sum_over(along[:, : 4 * width], "wsh")
    up_sum = along[0, 4 * width : 4 * width + up_bias.shape[0]]
    rms_values = jnp.sqrt(along[:, -3:] / (length * width))
    late = jnp.concatenate([sum_gain_one, sum_shift_one, qv_sum], axis=1)
    late = sum_over(sum_over(late, "ctx"), "wsh")

    def mine(vectors, at, size=shard):
        return lax.dynamic_slice_in_dim(vectors[0], at * width + wsh * size, size)

    return (
        block_full.astype(BF16)[None],
        input_grad[None],
        mine(late, 0),
        mine(late, 1),
        grad_qkv,
        mine(late, 2, 2 * shard),
        grad_out,
        mine(early, 2),
        mine(early, 0),
        mine(early, 1),
        grad_up,
        up_sum,
        grad_down,
        mine(early, 3),
        rms_values,
    )


def prefix(shard, axis, combine, identity):
    size, mine = (lax.axis_size(axis), lax.axis_index(axis))
    everything = lax.all_gather(shard, axis)
    start = jnp.broadcast_to(jnp.asarray(identity, shard.dtype), shard.shape)

    def step(k, before):
        reached = k < mine
        new = combine(before, everything[k])
        return jnp.where(reached, new, before)

    return lax.fori_loop(0, size, step, start)


def normed(values, gain, shift):
    centre = values - jnp.mean(values, axis=-1, keepdims=True)
    spread = jnp.mean(centre * centre, axis=-1, keepdims=True)
    return centre * lax.rsqrt(spread + EPSILON) * gain + shift


def gelu_tanh(values):
    return jax.nn.gelu(values, approximate=True)


def add_counts(earlier, later):
    return earlier + later


def allowed_pairs(query_segment, query_place, key_segment, key_place):
    return (
        (query_segment[:, None] == key_segment[None, :])
        & (key_place[None, :] <= query_place[:, None])
    )[:, None, :]


def score_pairs(query_rows, key_rows, scaling):
    return (
        jnp.einsum("qhd,khd->qhk", query_rows, key_rows, preferred_element_type=jnp.float32)
        * scaling
    )


def contract_rows(left, right):
    return lax.dot_general(
        left, right, (((0,), (0,)), ((), ())), preferred_element_type=jnp.float32
    )


def contract_cols(left, right):
    return lax.dot_general(
        left, right, (((1,), (1,)), ((), ())), preferred_element_type=jnp.float32
    )


def by_tokens(
    block_in,
    doc_flags,
    ln1_gain,
    ln1_bias,
    w_qkv,
    qv_bias,
    w_out,
    out_bias,
    ln2_gain,
    ln2_bias,
    w_up,
    up_bias,
    w_down,
    down_bias,
    cotangent,
):
    tok_rows = block_in.shape[1]
    model_width = block_in.shape[2]
    scaling = HD ** (-0.5)
    ctx_count = lax.axis_size("ctx")
    earlier = jnp.arange(tok_rows)
    running_count = jnp.sum(
        jnp.where(earlier[None, :] <= earlier[:, None], doc_flags[0][None, :], 0), axis=1
    )
    offset_count = prefix(running_count[-1], "ctx", add_counts, jnp.int32(0))
    local_segment = running_count + offset_count - 1
    local_place = lax.axis_index("ctx") * tok_rows + jnp.arange(tok_rows, dtype=jnp.int32)
    (
        gain_one,
        shift_one,
        qkv_full,
        qv_full,
        out_full,
        out_shift,
        gain_two,
        shift_two,
        up_full,
        up_shift,
        down_full,
        down_shift,
    ) = (
        lax.all_gather(ln1_gain, "wsh", axis=0, tiled=True),
        lax.all_gather(ln1_bias, "wsh", axis=0, tiled=True),
        lax.all_gather(w_qkv, "wsh", axis=0, tiled=True),
        lax.all_gather(qv_bias, "wsh", axis=0, tiled=True),
        lax.all_gather(w_out, "wsh", axis=0, tiled=True),
        lax.all_gather(out_bias, "wsh", axis=0, tiled=True),
        lax.all_gather(ln2_gain, "wsh", axis=0, tiled=True),
        lax.all_gather(ln2_bias, "wsh", axis=0, tiled=True),
        lax.all_gather(w_up, "wsh", axis=1, tiled=True),
        lax.all_gather(up_bias, "wsh", axis=0, tiled=True),
        lax.all_gather(w_down, "wsh", axis=0, tiled=True),
        lax.all_gather(down_bias, "wsh", axis=0, tiled=True),
    )
    gain_one, shift_one, gain_two, shift_two = [
        vector.astype(jnp.float32) for vector in (gain_one, shift_one, gain_two, shift_two)
    ]
    out_shift, up_shift, down_shift = [
        vector.astype(jnp.float32) for vector in (out_shift, up_shift, down_shift)
    ]
    input_rows = block_in[0].astype(jnp.float32)
    normed_one = normed(input_rows, gain_one, shift_one).astype(jnp.bfloat16)
    qkv_shift = jnp.concatenate(
        [qv_full[:model_width], jnp.zeros((model_width,), qv_full.dtype), qv_full[model_width:]]
    ).astype(jnp.float32)
    projected = (
        jnp.dot(normed_one, qkv_full, preferred_element_type=jnp.float32) + qkv_shift
    ).astype(jnp.bfloat16)
    queries = projected[:, :model_width].reshape(tok_rows, H, HD)
    key_rows = projected[:, model_width : 2 * model_width].reshape(tok_rows, H, HD)
    value_rows = projected[:, 2 * model_width :].reshape(tok_rows, H, HD)
    key_piece = lax.all_gather(key_rows, "ctx", axis=0, tiled=True)
    value_piece = lax.all_gather(value_rows, "ctx", axis=0, tiled=True)
    segment_piece = lax.all_gather(local_segment, "ctx", axis=0, tiled=True)
    piece_place = jnp.arange(key_piece.shape[0], dtype=jnp.int32)
    row_best = jnp.full((tok_rows, H), NEGATIVE, jnp.float32)
    score_block = score_pairs(queries, key_piece, scaling)
    allowed = allowed_pairs(local_segment, local_place, segment_piece, piece_place)
    new_best = jnp.maximum(row_best, jnp.max(jnp.where(allowed, score_block, NEGATIVE), axis=-1))
    weight_block = jnp.where(allowed, jnp.exp(score_block - new_best[..., None]), 0.0)
    row_total = jnp.sum(weight_block, axis=-1)
    weighted = jnp.einsum(
        "qhk,khd->qhd",
        weight_block.astype(jnp.bfloat16),
        value_piece,
        preferred_element_type=jnp.float32,
    )
    row_best, row_total, weighted = (new_best, row_total, weighted)
    log_total = row_best + jnp.log(row_total)
    attended = weighted / row_total[..., None]
    attended_low = attended.reshape(tok_rows, model_width).astype(jnp.bfloat16)
    attn_branch = jnp.dot(attended_low, out_full, preferred_element_type=jnp.float32) + out_shift
    residual = input_rows + attn_branch
    normed_two = normed(residual, gain_two, shift_two).astype(jnp.bfloat16)
    hidden_pre = jnp.dot(normed_two, up_full, preferred_element_type=jnp.float32) + up_shift
    hidden_act = gelu_tanh(hidden_pre).astype(jnp.bfloat16)
    mlp_sum = jnp.dot(hidden_act, down_full, preferred_element_type=jnp.float32)
    mlp_branch = mlp_sum + down_shift
    block_full = residual + mlp_branch
    square_sums = lax.psum(
        jnp.stack(
            [
                jnp.sum(attn_branch * attn_branch),
                jnp.sum(mlp_branch * mlp_branch),
                jnp.sum(block_full * block_full),
            ]
        ),
        "ctx",
    )
    rms_values = jnp.sqrt(square_sums / (tok_rows * ctx_count * model_width)).reshape(1, 3)
    out_grad = cotangent[0].astype(jnp.float32)
    mlp_grad = out_grad.astype(jnp.bfloat16)
    grad_down_shift = jnp.sum(mlp_grad.astype(jnp.float32), axis=0)
    grad_down = contract_rows(hidden_act, mlp_grad)
    act_grad = contract_cols(mlp_grad, down_full)
    unused_act, gelu_pull = jax.vjp(gelu_tanh, hidden_pre)
    pre_grad = gelu_pull(act_grad)[0].astype(jnp.bfloat16)
    grad_up_shift = jnp.sum(pre_grad.astype(jnp.float32), axis=0)
    grad_up = contract_rows(normed_two, pre_grad)
    normed_two_grad = contract_cols(pre_grad, up_full)
    unused_two, norm_two_pull = jax.vjp(normed, residual, gain_two, shift_two)
    residual_ln, grad_gain_two, grad_shift_two = norm_two_pull(normed_two_grad)
    residual_grad = out_grad + residual_ln
    attn_grad = residual_grad.astype(jnp.bfloat16)
    grad_out_shift = jnp.sum(attn_grad.astype(jnp.float32), axis=0)
    grad_out = contract_rows(attended_low, attn_grad)
    attended_grad = contract_cols(attn_grad, out_full).astype(jnp.bfloat16).reshape(tok_rows, H, HD)
    row_delta = jnp.sum(attended_grad.astype(jnp.float32) * attended, axis=-1)
    key_piece = lax.all_gather(key_rows, "ctx", axis=0, tiled=True)
    value_piece = lax.all_gather(value_rows, "ctx", axis=0, tiled=True)
    segment_piece = lax.all_gather(local_segment, "ctx", axis=0, tiled=True)
    piece_place = jnp.arange(key_piece.shape[0], dtype=jnp.int32)
    score_block = score_pairs(queries, key_piece, scaling)
    allowed = allowed_pairs(local_segment, local_place, segment_piece, piece_place)
    probability = jnp.where(allowed, jnp.exp(score_block - log_total[..., None]), 0.0)
    prob_grad = jnp.einsum(
        "qhd,khd->qhk", attended_grad, value_piece, preferred_element_type=jnp.float32
    )
    score_grad = (probability * (prob_grad - row_delta[..., None])).astype(jnp.bfloat16)
    query_grad = scaling * jnp.einsum(
        "qhk,khd->qhd", score_grad, key_piece, preferred_element_type=jnp.float32
    )
    query_piece = lax.all_gather(
        queries.astype(jnp.float32).astype(jnp.bfloat16), "ctx", axis=0, tiled=True
    ).astype(jnp.float32)
    grad_piece = lax.all_gather(
        attended_grad.astype(jnp.float32).astype(jnp.bfloat16), "ctx", axis=0, tiled=True
    )
    total_piece = lax.all_gather(log_total.astype(jnp.bfloat16), "ctx", axis=0, tiled=True).astype(
        jnp.float32
    )
    delta_piece = lax.all_gather(row_delta.astype(jnp.bfloat16), "ctx", axis=0, tiled=True).astype(
        jnp.float32
    )
    segment_piece = lax.all_gather(local_segment, "ctx", axis=0, tiled=True)
    query_low = query_piece.astype(jnp.bfloat16)
    piece_place = jnp.arange(query_piece.shape[0], dtype=jnp.int32)
    score_block = score_pairs(query_low, key_rows, scaling)
    allowed = allowed_pairs(segment_piece, piece_place, local_segment, local_place)
    probability = jnp.where(allowed, jnp.exp(score_block - total_piece[..., None]), 0.0)
    value_grad = jnp.einsum(
        "qhk,qhd->khd",
        probability.astype(jnp.bfloat16),
        grad_piece,
        preferred_element_type=jnp.float32,
    )
    prob_grad = jnp.einsum(
        "qhd,khd->qhk", grad_piece, value_rows, preferred_element_type=jnp.float32
    )
    score_grad = (probability * (prob_grad - delta_piece[..., None])).astype(jnp.bfloat16)
    key_grad = scaling * jnp.einsum(
        "qhk,qhd->khd", score_grad, query_low, preferred_element_type=jnp.float32
    )
    key_grad, value_grad = (key_grad, value_grad)
    qkv_grad = jnp.concatenate(
        [
            query_grad.reshape(tok_rows, model_width),
            key_grad.reshape(tok_rows, model_width),
            value_grad.reshape(tok_rows, model_width),
        ],
        axis=1,
    ).astype(jnp.bfloat16)
    qkv_grad_wide = qkv_grad.astype(jnp.float32)
    grad_qv_shift = jnp.concatenate(
        [
            jnp.sum(qkv_grad_wide[:, :model_width], axis=0),
            jnp.sum(qkv_grad_wide[:, 2 * model_width :], axis=0),
        ]
    )
    grad_qkv = contract_rows(normed_one, qkv_grad)
    normed_one_grad = contract_cols(qkv_grad, qkv_full)
    unused_one, norm_one_pull = jax.vjp(normed, input_rows, gain_one, shift_one)
    input_ln, grad_gain_one, grad_shift_one = norm_one_pull(normed_one_grad)
    input_grad = (residual_grad + input_ln).astype(jnp.bfloat16)
    (
        sum_gain_one,
        sum_shift_one,
        sum_qkv,
        sum_qv_shift,
        sum_out,
        sum_out_shift,
        sum_gain_two,
        sum_shift_two,
        sum_up,
        sum_up_shift,
        sum_down,
        sum_down_shift,
    ) = (
        lax.psum_scatter(
            grad_gain_one.astype(jnp.bfloat16), "wsh", scatter_dimension=0, tiled=True
        ).astype(jnp.float32),
        lax.psum_scatter(
            grad_shift_one.astype(jnp.bfloat16), "wsh", scatter_dimension=0, tiled=True
        ).astype(jnp.float32),
        lax.psum_scatter(
            grad_qkv.astype(jnp.bfloat16), "wsh", scatter_dimension=0, tiled=True
        ).astype(jnp.float32),
        lax.psum_scatter(
            grad_qv_shift.astype(jnp.bfloat16), "wsh", scatter_dimension=0, tiled=True
        ).astype(jnp.float32),
        lax.psum_scatter(
            grad_out.astype(jnp.bfloat16), "wsh", scatter_dimension=0, tiled=True
        ).astype(jnp.float32),
        lax.psum_scatter(
            grad_out_shift.astype(jnp.bfloat16), "wsh", scatter_dimension=0, tiled=True
        ).astype(jnp.float32),
        lax.psum_scatter(
            grad_gain_two.astype(jnp.bfloat16), "wsh", scatter_dimension=0, tiled=True
        ).astype(jnp.float32),
        lax.psum_scatter(
            grad_shift_two.astype(jnp.bfloat16), "wsh", scatter_dimension=0, tiled=True
        ).astype(jnp.float32),
        lax.psum_scatter(
            grad_up.astype(jnp.bfloat16), "wsh", scatter_dimension=1, tiled=True
        ).astype(jnp.float32),
        lax.psum_scatter(
            grad_up_shift.astype(jnp.bfloat16), "wsh", scatter_dimension=0, tiled=True
        ).astype(jnp.float32),
        lax.psum_scatter(
            grad_down.astype(jnp.bfloat16), "wsh", scatter_dimension=0, tiled=True
        ).astype(jnp.float32),
        lax.psum_scatter(
            grad_down_shift.astype(jnp.bfloat16), "wsh", scatter_dimension=0, tiled=True
        ).astype(jnp.float32),
    )
    totals = lax.psum(
        (
            sum_gain_one,
            sum_shift_one,
            sum_qkv,
            sum_qv_shift,
            sum_out,
            sum_out_shift,
            sum_gain_two,
            sum_shift_two,
            sum_up,
            sum_up_shift,
            sum_down,
            sum_down_shift,
        ),
        "ctx",
    )
    return (
        block_full.astype(jnp.bfloat16)[None],
        input_grad[None],
        totals[0],
        totals[1],
        totals[2],
        totals[3],
        totals[4],
        totals[5],
        totals[6],
        totals[7],
        totals[8],
        totals[9],
        totals[10],
        totals[11],
        rms_values,
    )


def solution(mesh):
    each = LANES // HD
    by_head = mesh.shape["ctx"] == 8 and mesh.shape["ctx"] * each + 1 == H and mesh.shape["wsh"] == 4
    return jax.shard_map(
        by_heads if by_head else by_tokens,
        mesh=mesh,
        in_specs=(
            P("wsh", "ctx", None),
            P("wsh", "ctx"),
            P("wsh"),
            P("wsh"),
            P("wsh", None),
            P("wsh"),
            P("wsh", None),
            P("wsh"),
            P("wsh"),
            P("wsh"),
            P(None, "wsh"),
            P("wsh"),
            P("wsh", None),
            P("wsh"),
            P("wsh", "ctx", None),
        ),
        out_specs=(
            P("wsh", "ctx", None),
            P("wsh", "ctx", None),
            P("wsh"),
            P("wsh"),
            P("wsh", None),
            P("wsh"),
            P("wsh", None),
            P("wsh"),
            P("wsh"),
            P("wsh"),
            P(None, "wsh"),
            P("wsh"),
            P("wsh", None),
            P("wsh"),
            P("wsh", None),
        ),
        check_vma=False,
    )
```

```python
import functools
import math

import jax
import jax.numpy as jnp
from jax import lax
from jax.experimental import pallas as pl
from jax.experimental.pallas import tpu as pltpu
from jax.sharding import PartitionSpec as P

H = 17
HD = 64
LANES = 128
EPSILON = 1e-05
NEGATIVE = -1e30
LOG2E = math.log2(math.e)
SCORE_SCALE = HD ** (-0.5) * LOG2E
VMEM_MOST = 56 * 2**20

F32 = jnp.float32
BF16 = jnp.bfloat16


def dot_nn(left, right):
    return lax.dot_general(left, right, (((1,), (0,)), ((), ())), preferred_element_type=F32)


def dot_nt(left, right):
    return lax.dot_general(left, right, (((1,), (1,)), ((), ())), preferred_element_type=F32)


def dot_tn(left, right):
    return lax.dot_general(left, right, (((0,), (0,)), ((), ())), preferred_element_type=F32)


def swap(value, axis, distance):
    size = lax.axis_size(axis)
    return lax.ppermute(value, axis, [(i, i ^ distance) for i in range(size)])


def centred(values):
    centre = values - jnp.mean(values, axis=-1, keepdims=True)
    spread = jnp.mean(centre * centre, axis=-1, keepdims=True)
    return centre, lax.rsqrt(spread + EPSILON)


def norm_back(unit, inverse, scaled_grad):
    mean_grad = jnp.mean(scaled_grad, axis=-1, keepdims=True)
    mean_both = jnp.mean(scaled_grad * unit, axis=-1, keepdims=True)
    return inverse * (scaled_grad - mean_grad - unit * mean_both)


VECTORS = 8
VECTOR_ROWS = {
    "gain_one": 0,
    "shift_one": 1,
    "out_shift": 4,
    "gain_two": 5,
    "shift_two": 6,
    "down_shift": 7,
}


def row_of(vector_ref, name):
    return vector_ref[pl.ds(VECTOR_ROWS[name], 1), :]


class Order:
    def __init__(self, place):
        self.place = place

    def wait(self, *values):
        self.place = after(self.place, *values)


def after(value, *others):
    return lax.optimization_barrier((value, *others))[0]


def whole_call(kernel, name, shapes, scratch, flops, order, *arrays):
    moved = sum(a.size * a.dtype.itemsize for a in arrays)
    moved += sum(math.prod(s.shape) * s.dtype.itemsize for s in shapes)
    outs = pl.pallas_call(
        kernel,
        out_shape=shapes,
        in_specs=[pl.BlockSpec(memory_space=pltpu.SMEM)]
        + [pl.BlockSpec(memory_space=pltpu.VMEM)] * len(arrays),
        out_specs=[pl.BlockSpec(memory_space=pltpu.VMEM)] * len(shapes),
        scratch_shapes=scratch,
        compiler_params=pltpu.CompilerParams(vmem_limit_bytes=VMEM_MOST),
        cost_estimate=pl.CostEstimate(flops=flops, bytes_accessed=moved, transcendentals=0),
        name=name,
    )(order.place, *arrays)
    order.wait(outs[0])
    return outs


QB = 256


def head_lanes(head):
    lane = lax.broadcasted_iota(jnp.int32, (1, LANES), 1)
    return (lane >= HD * head) & (lane < HD * (head + 1))


def masked_scores(keys, queries, start_row, key_at, query_at):
    scores = dot_nt(keys, queries) * SCORE_SCALE
    shape = scores.shape
    key_place = lax.broadcasted_iota(jnp.int32, shape, 0) + key_at
    allowed = key_place >= start_row
    if key_at + shape[0] > query_at:
        query_place = lax.broadcasted_iota(jnp.int32, shape, 1) + query_at
        allowed = allowed & (key_place <= query_place)
    return jnp.where(allowed, scores, NEGATIVE)


def fold_rows(values, combine):
    return combine(values.reshape(values.shape[0] // 8, 8, values.shape[1]), axis=0)


def attend_forward_kernel(
    n_ctx, n_wsh, place_ref, start_ref, vector_ref, bias_ref, *refs
):
    blocks, refs = refs[:n_ctx], refs[n_ctx:]
    weights, refs = refs[:n_wsh], refs[n_wsh:]
    normed_ref, qkv_ref, attended_ref, total_ref, own_ref, low_ref, *refs = refs
    weight_ref, score_ref, prob_ref, value_ref = refs
    ctx, wsh = place_ref[0], place_ref[1]
    tok_rows = blocks[0].shape[0]
    length = n_ctx * tok_rows
    weight_rows = weight_ref.shape[0] // n_wsh
    for k in range(n_wsh):
        at = pl.multiple_of((wsh ^ k) * weight_rows, 16)
        weight_ref[pl.ds(at, weight_rows), :] = weights[k][pl.ds(0, weight_rows), :]
    for j in range(n_ctx):
        at = pl.multiple_of((ctx ^ j) * tok_rows, tok_rows)
        centre, inverse = centred(blocks[j][...].astype(F32))
        values = centre * inverse * row_of(vector_ref, "gain_one") + row_of(vector_ref, "shift_one")
        normed_ref[pl.ds(at, tok_rows), :] = values.astype(BF16)
    for at in range(0, length, QB):
        rows = pl.ds(at, QB)
        values = dot_nn(normed_ref[rows, :], weight_ref[...]) + bias_ref[...]
        qkv_ref[rows, :] = values.astype(BF16)
    for group in range(2):
        value_ref[group] = qkv_ref[:, pl.ds((4 + group) * LANES, LANES)].T
    for head in range(3):
        group, half = head // 2, head % 2
        for query_at in range(0, length, QB):
            columns = pl.ds(query_at, QB)
            queries = qkv_ref[columns, pl.ds(group * LANES, LANES)]
            queries = jnp.where(head_lanes(half), queries, 0)
            start_row = start_ref[:, columns]
            best = None
            for key_at in range(0, query_at + QB, QB):
                keys = qkv_ref[pl.ds(key_at, QB), pl.ds((2 + group) * LANES, LANES)]
                scores = masked_scores(keys, queries, start_row, key_at, query_at)
                score_ref[pl.ds(key_at, QB), :] = scores
                most = fold_rows(scores, jnp.max)
                best = most if best is None else jnp.maximum(best, most)
            best = jnp.max(best, axis=0, keepdims=True)
            total = None
            for key_at in range(0, query_at + QB, QB):
                weight = jnp.exp2(score_ref[pl.ds(key_at, QB), :] - best)
                some = fold_rows(weight, jnp.sum)
                total = some if total is None else total + some
                prob_ref[pl.ds(key_at, QB), :] = weight.astype(BF16)
            total = jnp.sum(total, axis=0, keepdims=True)
            reach = query_at + QB
            values = value_ref[group, pl.ds(half * HD, HD), pl.ds(0, reach)]
            weighted = dot_nn(values, prob_ref[pl.ds(0, reach), :])
            attended_ref[pl.ds(head * HD, HD), columns] = weighted / total
            total_ref[pl.ds(head, 1), columns] = best + jnp.log2(total)
            if half == 1:
                low_ref[columns, :] = attended_ref[pl.ds(0, 2 * HD), columns].T.astype(BF16)
    at = pl.multiple_of(ctx * tok_rows, tok_rows)
    shared = attended_ref[pl.ds(2 * HD, HD), pl.ds(at, tok_rows)]
    shared = jnp.concatenate([shared, jnp.zeros_like(shared)], axis=0)
    own_ref[...] = shared.T.astype(BF16)


def attend_forward(order, start_row, vectors, bias, blocks, weights):
    n_ctx, n_wsh = len(blocks), len(weights)
    tok_rows, width = blocks[0].shape
    length = n_ctx * tok_rows
    columns = weights[0].shape[1]
    pairs = 3 * length * length // 2
    return whole_call(
        functools.partial(attend_forward_kernel, n_ctx, n_wsh),
        "attend_forward",
        [
            jax.ShapeDtypeStruct((length, width), BF16),
            jax.ShapeDtypeStruct((length, columns), BF16),
            jax.ShapeDtypeStruct((3 * HD, length), F32),
            jax.ShapeDtypeStruct((8, length), F32),
            jax.ShapeDtypeStruct((tok_rows, LANES), BF16),
            jax.ShapeDtypeStruct((length, LANES), BF16),
        ],
        [
            pltpu.VMEM((width, columns), BF16),
            pltpu.VMEM((length, QB), F32),
            pltpu.VMEM((length, QB), BF16),
            pltpu.VMEM((2, LANES, length), BF16),
        ],
        2 * length * width * columns + 4 * pairs * LANES,
        order,
        start_row,
        vectors,
        bias,
        *blocks,
        *weights,
    )


def attend_backward_kernel(
    place_ref,
    start_ref,
    qkv_ref,
    attended_ref,
    total_ref,
    grad_ref,
    all_ref,
    own_ref,
    send_ref,
    key_ref,
    turned_ref,
    sum_ref,
    query_ref,
):
    length, tok_rows = qkv_ref.shape[0], own_ref.shape[0]
    for group in range(2):
        key_ref[group] = qkv_ref[:, pl.ds((2 + group) * LANES, LANES)].T
        turned_ref[group] = grad_ref[:, pl.ds(group * LANES, LANES)].T
    sum_ref[...] = jnp.zeros_like(sum_ref)
    for head in range(3):
        group, half = head // 2, head % 2
        for query_at in range(0, length, QB):
            columns = pl.ds(query_at, QB)
            lanes = head_lanes(half)
            queries = qkv_ref[columns, pl.ds(group * LANES, LANES)]
            queries = jnp.where(lanes, queries, 0)
            grad = jnp.where(lanes, grad_ref[columns, pl.ds(group * LANES, LANES)], 0)
            start_row = start_ref[:, columns]
            total = total_ref[pl.ds(head, 1), columns]
            turned = turned_ref[group, pl.ds(half * HD, HD), columns].astype(F32)
            delta = turned * attended_ref[pl.ds(head * HD, HD), columns]
            delta = jnp.sum(delta, axis=0, keepdims=True)
            query_grad = None
            for key_at in range(0, query_at + QB, QB):
                rows = pl.ds(key_at, QB)
                keys = qkv_ref[rows, pl.ds((2 + group) * LANES, LANES)]
                values = qkv_ref[rows, pl.ds((4 + group) * LANES, LANES)]
                scores = masked_scores(keys, queries, start_row, key_at, query_at)
                prob = jnp.exp2(scores - total)
                score_grad = (prob * (dot_nt(values, grad) - delta)).astype(BF16)
                sum_ref[1, rows, pl.ds(group * LANES, LANES)] += dot_nn(prob.astype(BF16), grad)
                sum_ref[0, rows, pl.ds(group * LANES, LANES)] += dot_nn(score_grad, queries)
                part = dot_nn(key_ref[group, pl.ds(half * HD, HD), rows], score_grad)
                query_grad = part if query_grad is None else query_grad + part
            query_ref[pl.ds(head * HD, HD), columns] = query_grad * HD ** (-0.5)
    query_ref[pl.ds(3 * HD, HD), :] = jnp.zeros((HD, length), F32)
    for group in range(2):
        lanes = pl.ds(group * LANES, LANES)
        all_ref[:, lanes] = query_ref[pl.ds(group * LANES, LANES), :].T.astype(BF16)
        key_grad = sum_ref[0, :, lanes] * HD ** (-0.5)
        all_ref[:, pl.ds((2 + group) * LANES, LANES)] = key_grad.astype(BF16)
        all_ref[:, pl.ds((4 + group) * LANES, LANES)] = sum_ref[1, :, lanes].astype(BF16)
    at = pl.multiple_of(place_ref[0] * tok_rows, tok_rows)
    for part in range(3):
        lanes = pl.ds(part * LANES, LANES)
        send_ref[:, lanes] = all_ref[:, pl.ds(2 * part * LANES, LANES)]
        own_ref[:, lanes] = all_ref[pl.ds(at, tok_rows), pl.ds((2 * part + 1) * LANES, LANES)]


def attend_backward(order, start_row, qkv, attended, total, grad, tok_rows):
    length = grad.shape[0]
    pairs = 3 * length * length // 2
    shapes = [
        jax.ShapeDtypeStruct((length, 6 * LANES), BF16),
        jax.ShapeDtypeStruct((tok_rows, 3 * LANES), BF16),
        jax.ShapeDtypeStruct((length, 3 * LANES), BF16),
    ]
    scratch = [
        pltpu.VMEM((2, LANES, length), BF16),
        pltpu.VMEM((2, LANES, length), BF16),
        pltpu.VMEM((2, length, 2 * LANES), F32),
        pltpu.VMEM((2 * LANES, length), F32),
    ]
    return whole_call(
        attend_backward_kernel,
        "attend_backward",
        shapes,
        scratch,
        10 * pairs * LANES,
        order,
        start_row,
        qkv,
        attended,
        total,
        grad,
    )


SPARE = 16


def take_columns_kernel(place_ref, weight_ref, vector_ref, out_ref):
    rows, width = weight_ref.shape[0], weight_ref.shape[1] // 3
    ctx = place_ref[0]
    out_ref[...] = jnp.zeros_like(out_ref)
    top = pl.ds(0, rows)
    for kind in range(3):
        at = kind * width
        shared = weight_ref[:, pl.ds(at + width - HD, HD)]
        start = at // LANES * LANES
        span = LANES if at == start else 2 * LANES
        pair = weight_ref[:, pl.ds(pl.multiple_of(start + ctx * LANES, LANES), span)]
        out_ref[top, pl.ds(2 * kind * LANES, LANES)] = pair[:, at - start : at - start + LANES]
        out_ref[top, pl.ds((2 * kind + 1) * LANES, HD)] = shared
    out_ref[pl.ds(rows, VECTORS), pl.ds(0, vector_ref.shape[1])] = vector_ref[...]


def take_columns(order, weight, vectors):
    shape = jax.ShapeDtypeStruct((weight.shape[0] + 16, 6 * LANES), BF16)
    return whole_call(take_columns_kernel, "take_columns", [shape], [], 0, order, weight, vectors)[0]


def lay_weight(weight_ref, parts, wsh):
    rows = parts[0].shape[0]
    for k, part in enumerate(parts):
        weight_ref[pl.ds(pl.multiple_of((wsh ^ k) * rows, 16), rows), :] = part[...]


def out_project_kernel(n_wsh, place_ref, own_ref, in_ref, vector_ref, part_ref, *refs):
    weights, refs = refs[:n_wsh], refs[n_wsh:]
    low_refs, (residual_ref, normed_ref, square_ref, weight_ref, low_ref) = refs[:n_wsh], refs[n_wsh:]
    tok_rows = own_ref.shape[0]
    n_parts = part_ref.shape[0] // tok_rows
    lay_weight(weight_ref, weights, place_ref[1])
    for i in range(n_parts):
        low_ref[:, pl.ds(i * LANES, LANES)] = part_ref[pl.ds(i * tok_rows, tok_rows), :]
    low_ref[:, pl.ds(n_parts * LANES, HD)] = own_ref[:, pl.ds(0, HD)]
    branch = dot_nn(low_ref[...], weight_ref[...]) + row_of(vector_ref, "out_shift")
    square_ref[...] = jnp.broadcast_to(jnp.sum(branch * branch), square_ref.shape)
    residual = in_ref[...].astype(F32) + branch
    residual_ref[...] = residual
    centre, inverse = centred(residual)
    values = centre * inverse * row_of(vector_ref, "gain_two") + row_of(vector_ref, "shift_two")
    normed_ref[...] = values.astype(BF16)
    shard = low_refs[0].shape[1]
    attended = low_ref[...].astype(F32)
    for k, out_ref in enumerate(low_refs):
        columns = 0.0
        for i in range(n_wsh):
            chosen = (place_ref[1] ^ k) == i
            columns = jnp.where(chosen, attended[:, i * shard : (i + 1) * shard], columns)
        out_ref[...] = columns.astype(BF16)


def out_project(order, own, rows_in, vectors, parts, weights):
    tok_rows, width = rows_in.shape
    return whole_call(
        functools.partial(out_project_kernel, len(weights)),
        "out_project",
        [jax.ShapeDtypeStruct((tok_rows, width // len(weights)), BF16)] * len(weights)
        + [
            jax.ShapeDtypeStruct((tok_rows, width), F32),
            jax.ShapeDtypeStruct((tok_rows, width), BF16),
            jax.ShapeDtypeStruct((1, LANES), F32),
        ],
        [pltpu.VMEM((width, width), BF16), pltpu.VMEM((tok_rows, width), BF16)],
        2 * tok_rows * width * width,
        order,
        own,
        rows_in,
        vectors,
        parts,
        *weights,
    )


def act_back_kernel(place_ref, *refs):
    *grads, down_ref, near_ref, far_ref = refs
    tok_rows = grads[0].shape[0]
    for k, grad in enumerate(grads):
        out_ref = near_ref if k < 2 else far_ref
        out_ref[pl.ds(k % 2 * tok_rows, tok_rows), :] = dot_nt(grad[...], down_ref[...])


def act_back(order, grads, down):
    tok_rows, width = grads[0].shape
    units = down.shape[0]
    return whole_call(
        act_back_kernel,
        "act_back",
        [
            jax.ShapeDtypeStruct((2 * tok_rows, units), F32),
            jax.ShapeDtypeStruct((2 * tok_rows, units), F32),
        ],
        [],
        2 * 4 * tok_rows * width * units,
        order,
        *grads,
        down,
    )


GELU_SLOPE = math.sqrt(2 / math.pi)
GELU_CUBE = 0.044715


def feed_kernel(
    place_ref,
    first_ref,
    second_ref,
    grad_ref,
    up_ref,
    bias_ref,
    act_ref,
    pre_ref,
    first_back_ref,
    second_back_ref,
    shift_ref,
    rows_ref,
):
    tok_rows = first_ref.shape[0]
    rows_ref[pl.ds(0, tok_rows), :] = first_ref[...]
    rows_ref[pl.ds(tok_rows, tok_rows), :] = second_ref[...]
    hidden = dot_nn(rows_ref[...], up_ref[...]) + bias_ref[...]
    square = hidden * hidden
    turn = jnp.tanh(hidden * (GELU_SLOPE + GELU_SLOPE * GELU_CUBE * square))
    half = 0.5 + 0.5 * turn
    act_ref[...] = (hidden * half).astype(BF16)
    slope = half + 0.5 * hidden * (1.0 - turn * turn) * (
        GELU_SLOPE + 3 * GELU_SLOPE * GELU_CUBE * square
    )
    pre = (grad_ref[...] * slope).astype(BF16)
    pre_ref[...] = pre
    shift_ref[...] = jnp.sum(pre.astype(F32), axis=0, keepdims=True)
    back = dot_nt(pre, up_ref[...])
    first_back_ref[...] = back[:tok_rows]
    second_back_ref[...] = back[tok_rows:].astype(BF16)


def feed(order, first, second, grad, up, bias, name):
    tok_rows, width = first.shape
    units = up.shape[1]
    return whole_call(
        feed_kernel,
        name,
        [
            jax.ShapeDtypeStruct((2 * tok_rows, units), BF16),
            jax.ShapeDtypeStruct((2 * tok_rows, units), BF16),
            jax.ShapeDtypeStruct((tok_rows, width), F32),
            jax.ShapeDtypeStruct((tok_rows, width), BF16),
            jax.ShapeDtypeStruct((1, units), F32),
        ],
        [pltpu.VMEM((2 * tok_rows, width), BF16)],
        8 * tok_rows * width * units,
        order,
        first,
        second,
        grad,
        up,
        bias,
    )


def feed_out_kernel(place_ref, near_ref, far_ref, down_ref, own_ref, across_ref, send_ref):
    tok_rows = own_ref.shape[0]
    for k, (act_ref, out_ref) in enumerate(((near_ref, own_ref), (far_ref, across_ref))):
        values = dot_nn(act_ref[...], down_ref[...])
        out_ref[...] = values[:tok_rows]
        send_ref[k] = values[tok_rows:].astype(BF16)


def feed_out(order, near, far, down):
    tok_rows, width = near.shape[0] // 2, down.shape[1]
    return whole_call(
        feed_out_kernel,
        "feed_out",
        quarter_shapes(tok_rows, width),
        [],
        8 * tok_rows * width * down.shape[0],
        order,
        near,
        far,
        down,
    )


def block_sum_kernel(
    place_ref, residual_ref, own_ref, near_ref, across_ref, vector_ref, out_ref, square_ref
):
    branch = own_ref[...] + near_ref[0].astype(F32) + across_ref[...].astype(F32)
    branch = branch + row_of(vector_ref, "down_shift")
    total = residual_ref[...] + branch
    out_ref[...] = total.astype(BF16)
    square_ref[pl.ds(0, 1), :] = jnp.broadcast_to(jnp.sum(branch * branch), (1, LANES))
    square_ref[pl.ds(1, 1), :] = jnp.broadcast_to(jnp.sum(total * total), (1, LANES))


def block_sum(order, residual, own, near, across, vectors):
    tok_rows, width = residual.shape
    shapes = [
        jax.ShapeDtypeStruct((tok_rows, width), BF16),
        jax.ShapeDtypeStruct((2, LANES), F32),
    ]
    return whole_call(
        block_sum_kernel, "block_sum", shapes, [], 0, order, residual, own, near, across, vectors
    )


def residual_back_kernel(
    n_wsh, place_ref, own_ref, near_ref, across_ref, residual_ref, cotangent_ref, vector_ref, *refs
):
    weights, refs = refs[:n_wsh], refs[n_wsh:]
    total_ref, low_ref, send_ref, weight_ref = refs
    tok_rows = total_ref.shape[0]
    n_parts = send_ref.shape[0] // tok_rows
    lay_weight(weight_ref, weights, place_ref[1])
    grad = own_ref[...] + near_ref[...].astype(F32) + across_ref[...].astype(F32)
    centre, inverse = centred(residual_ref[...])
    unit = centre * inverse
    sums = [jnp.sum(values, axis=0, keepdims=True) for values in (grad * unit, grad)]
    sums.append(jnp.zeros((SPARE - 2, grad.shape[1]), F32))
    scaled = grad * row_of(vector_ref, "gain_two")
    total = cotangent_ref[...].astype(F32) + norm_back(unit, inverse, scaled)
    total_ref[...] = total
    low = total.astype(BF16)
    low_ref[pl.ds(0, tok_rows), :] = low
    low_ref[pl.ds(tok_rows, SPARE), :] = jnp.concatenate(sums, axis=0).astype(BF16)
    back = dot_nt(low, weight_ref[...]).astype(BF16)
    shared = back[:, n_parts * LANES :]
    shared = jnp.concatenate([shared, jnp.zeros_like(shared)], axis=1)
    for i in range(n_parts):
        rows = pl.ds(i * tok_rows, tok_rows)
        send_ref[rows, pl.ds(0, LANES)] = back[:, i * LANES : (i + 1) * LANES]
        send_ref[rows, pl.ds(LANES, LANES)] = shared


def residual_back(order, own, near, across, residual, cotangent, vectors, weights, n_ctx):
    tok_rows, width = residual.shape
    return whole_call(
        functools.partial(residual_back_kernel, len(weights)),
        "residual_back",
        [
            jax.ShapeDtypeStruct((tok_rows, width), F32),
            jax.ShapeDtypeStruct((tok_rows + SPARE, width), BF16),
            jax.ShapeDtypeStruct((n_ctx * tok_rows, 2 * LANES), BF16),
        ],
        [pltpu.VMEM((width, width), BF16)],
        2 * tok_rows * width * width,
        order,
        own,
        near,
        across,
        residual,
        cotangent,
        vectors,
        *weights,
    )


def input_back_kernel(n_wsh, place_ref, own_ref, in_ref, total_ref, vector_ref, part_ref, *refs):
    weights, refs = refs[:n_wsh], refs[n_wsh:]
    back_ref, weight_ref, grad_ref = refs
    tok_rows, width = back_ref.shape
    weight_rows = weights[0].shape[0]
    n_parts = part_ref.shape[0] // tok_rows
    grad = 0.0
    for kind in range(3):
        for k in range(n_wsh):
            at = pl.multiple_of((place_ref[1] ^ k) * weight_rows, 16)
            columns = pl.ds(kind * width, width)
            weight_ref[pl.ds(at, weight_rows), :] = weights[k][:, columns]
        for i in range(n_parts):
            part = part_ref[pl.ds(i * tok_rows, tok_rows), pl.ds(kind * LANES, LANES)]
            grad_ref[:, pl.ds(i * LANES, LANES)] = part
        grad_ref[:, pl.ds(n_parts * LANES, HD)] = own_ref[:, pl.ds(kind * LANES, HD)]
        grad = grad + dot_nt(grad_ref[...], weight_ref[...])
    centre, inverse = centred(in_ref[...].astype(F32))
    unit = centre * inverse
    total = total_ref[...] + norm_back(unit, inverse, grad * row_of(vector_ref, "gain_one"))
    back_ref[...] = total.astype(BF16)


def input_back(order, own, rows_in, total, vectors, parts, weights):
    tok_rows, width = rows_in.shape
    return whole_call(
        functools.partial(input_back_kernel, len(weights)),
        "input_back",
        [jax.ShapeDtypeStruct((tok_rows, width), BF16)],
        [pltpu.VMEM((width, width), BF16), pltpu.VMEM((tok_rows, width), BF16)],
        6 * tok_rows * width * width,
        order,
        own,
        rows_in,
        total,
        vectors,
        parts,
        *weights,
    )[0]


def join_rows(whole_ref, parts):
    at = 0
    for part in parts:
        whole_ref[pl.ds(at, part.shape[0]), :] = part[...]
        at += part.shape[0]


def weight_grad(full_ref, left_ref, right_ref):
    columns = left_ref.shape[1]
    for at in range(0, columns, 256):
        some = pl.ds(at, min(256, columns - at))
        full_ref[some, :] = dot_tn(left_ref[:, some], right_ref[...])


def split_halves(place_ref, full_ref, send_ref, keep_ref):
    far, rows = send_ref.shape[:2]
    near = place_ref[0] & 1
    for i in range(far):
        at = pl.multiple_of((2 * i + near) * rows, 8)
        keep_ref[i] = full_ref[pl.ds(at, rows), :].astype(BF16)
        at = pl.multiple_of((2 * i + 1 - near) * rows, 8)
        send_ref[i] = full_ref[pl.ds(at, rows), :].astype(BF16)


def split_parts(place_ref, full_ref, first_ref, second_ref, keep_ref):
    rows = keep_ref.shape[1]
    near, far = place_ref[0] & 1, place_ref[0] >> 1
    for k in range(4):
        at = pl.multiple_of((2 * (far ^ k) + near) * rows, 8)
        keep_ref[k] = full_ref[pl.ds(at, rows), :].astype(BF16)
        at = pl.multiple_of((2 * (far ^ k) + 1 - near) * rows, 8)
        out = first_ref if k % 2 else second_ref
        out[k // 2] = full_ref[pl.ds(at, rows), :].astype(BF16)


def halves_shapes(rows, width):
    pair = jax.ShapeDtypeStruct((2, rows // 8, width), BF16)
    return [pair, pair, jax.ShapeDtypeStruct((4, rows // 8, width), BF16)]


def grad_halves_kernel(n_left, n_right, place_ref, *refs):
    lefts, refs = refs[:n_left], refs[n_left:]
    rights, refs = refs[:n_right], refs[n_right:]
    send_ref, keep_ref, left_ref, right_ref, full_ref = refs
    join_rows(left_ref, lefts)
    join_rows(right_ref, rights)
    weight_grad(full_ref, left_ref, right_ref)
    split_halves(place_ref, full_ref, send_ref, keep_ref)


def grad_halves(order, lefts, rights, name):
    tokens = sum(part.shape[0] for part in lefts)
    units, width = lefts[0].shape[1], rights[0].shape[1]
    pieces = jax.ShapeDtypeStruct((4, units // 8, width), BF16)
    return whole_call(
        functools.partial(grad_halves_kernel, len(lefts), len(rights)),
        name,
        [pieces, pieces],
        [
            pltpu.VMEM((tokens, units), BF16),
            pltpu.VMEM((tokens, width), BF16),
            pltpu.VMEM((units, width), F32),
        ],
        2 * tokens * units * width,
        order,
        *lefts,
        *rights,
    )


def split_quarters(place_ref, full_ref, own_ref, across_ref, send_ref, rows, below):
    for k in range(4):
        at = pl.multiple_of((place_ref[1] ^ k) * rows, 8)
        values = jnp.concatenate([full_ref[pl.ds(at, rows), :], below(k)], axis=0)
        if k % 2:
            send_ref[k // 2] = values.astype(BF16)
        else:
            (across_ref if k else own_ref)[...] = values


def quarter_shapes(rows, width):
    wide = jax.ShapeDtypeStruct((rows, width), F32)
    return [wide, wide, jax.ShapeDtypeStruct((2, rows, width), BF16)]


def grad_qkv_kernel(place_ref, left_ref, right_ref, *refs):
    *outs, full_ref = refs
    weight_grad(full_ref, left_ref, right_ref)
    rows = left_ref.shape[1] // 4
    sums = jnp.sum(right_ref[...].astype(F32), axis=0, keepdims=True)
    below = jnp.broadcast_to(sums, (outs[0].shape[0] - rows, sums.shape[1]))
    split_quarters(place_ref, full_ref, *outs, rows, lambda k: below)


def grad_qkv_quarters(order, left, right):
    tokens, units = left.shape
    width = right.shape[1]
    return whole_call(
        grad_qkv_kernel,
        "grad_qkv",
        quarter_shapes(units // 4 + SPARE, width),
        [pltpu.VMEM((units, width), F32)],
        2 * tokens * units * width,
        order,
        left,
        right,
    )


def down_halves_kernel(n_act, n_wsh, place_ref, near_sum_ref, far_sum_ref, *refs):
    acts, refs = refs[:n_act], refs[n_act:]
    grads, refs = refs[:n_wsh], refs[n_wsh:]
    lows, refs = refs[:n_wsh], refs[n_wsh:]
    backs, refs = refs[:n_wsh], refs[n_wsh:]
    *outs, act_ref, low_ref, right_ref, full_ref = refs
    units, shard = act_ref.shape[1], low_ref.shape[1]
    tok_rows, width = grads[0].shape
    join_rows(act_ref, acts)
    join_rows(right_ref, grads)
    weight_grad(full_ref, act_ref, right_ref)
    sums = [jnp.sum(right_ref[...].astype(F32), axis=0, keepdims=True)]
    join_rows(low_ref, lows)
    for k, back in enumerate(backs):
        right_ref[pl.ds(k * tok_rows, tok_rows), :] = back[pl.ds(0, tok_rows), :]
    weight_grad(full_ref.at[pl.ds(units, shard), :], low_ref, right_ref)
    sums.append(jnp.sum(right_ref[...].astype(F32), axis=0, keepdims=True))
    sums.append(sum(back[pl.ds(tok_rows, SPARE), :].astype(F32) for back in backs)[:2])
    sums.append(near_sum_ref[...] + far_sum_ref[...])
    spare = full_ref.shape[0] - units - shard
    sums.append(jnp.zeros((spare - 5, width), F32))
    full_ref[pl.ds(units + shard, spare), :] = jnp.concatenate(sums, axis=0)
    (split_parts if len(outs) == 3 else split_halves)(place_ref, full_ref, *outs)


def down_halves(order, near_sum, far_sum, acts, grads, lows, backs, in_parts):
    tokens = sum(part.shape[0] for part in acts)
    units, shard, width = acts[0].shape[1], lows[0].shape[1], grads[0].shape[1]
    rows = -(-(units + shard + 8) // 128) * 128
    pieces = jax.ShapeDtypeStruct((4, rows // 8, width), BF16)
    return whole_call(
        functools.partial(down_halves_kernel, len(acts), len(grads)),
        "grad_down",
        halves_shapes(rows, width) if in_parts else [pieces, pieces],
        [
            pltpu.VMEM((tokens, units), BF16),
            pltpu.VMEM((tokens, shard), BF16),
            pltpu.VMEM((tokens, width), BF16),
            pltpu.VMEM((rows, width), F32),
        ],
        2 * tokens * (units + shard) * width,
        order,
        near_sum,
        far_sum,
        *acts,
        *grads,
        *lows,
        *backs,
    )


def qkv_piece_kernel(
    place_ref, own_ref, near_ref, across_ref, first_ref, square_ref, pair_ref, shared_ref
):
    squares = (first_ref[...], square_ref[pl.ds(0, 1), :], square_ref[pl.ds(1, 1), :])
    rows = own_ref.shape[0] - SPARE
    at_row = lax.broadcasted_iota(jnp.int32, (SPARE, LANES), 0)
    for kind in range(3):
        to = pl.ds(kind * LANES, LANES)
        for side, out in enumerate((pair_ref, shared_ref)):
            lanes = pl.ds((2 * kind + side) * LANES, LANES)
            total = own_ref[:, lanes] + near_ref[0, :, lanes].astype(F32)
            out[:, to] = (total + across_ref[:, lanes].astype(F32)).astype(BF16)
        last = pl.ds(rows, SPARE)
        values = jnp.where(at_row == 1, squares[kind], pair_ref[last, to].astype(F32))
        pair_ref[last, to] = values.astype(BF16)


def qkv_piece(order, own, near, across, first, squares):
    shape = jax.ShapeDtypeStruct((own.shape[0], 3 * LANES), BF16)
    return whole_call(
        qkv_piece_kernel,
        "qkv_piece",
        [shape, shape],
        [],
        0,
        order,
        own,
        near,
        across,
        first,
        squares,
    )


def half_sum_kernel(place_ref, keep_ref, got_ref, send_ref, own_ref):
    far = place_ref[0] >> 1
    for k in range(2):
        at = far ^ (2 * k)
        own_ref[k] = (keep_ref[at].astype(F32) + got_ref[at].astype(F32)).astype(BF16)
        at = far ^ (2 * k + 1)
        send_ref[k] = (keep_ref[at].astype(F32) + got_ref[at].astype(F32)).astype(BF16)


def half_sum(order, keep, got):
    pieces = jax.ShapeDtypeStruct((2, *keep.shape[1:]), BF16)
    return whole_call(half_sum_kernel, "half_sum", [pieces, pieces], [], 0, order, keep, got)


def pair_sum_kernel(place_ref, keep_ref, got_ref, send_ref, own_ref):
    send_ref[...] = (keep_ref[1].astype(F32) + got_ref[1].astype(F32)).astype(BF16)
    own_ref[...] = keep_ref[0].astype(F32) + got_ref[0].astype(F32)


def pair_sum(order, keep, got):
    shapes = [jax.ShapeDtypeStruct(keep.shape[1:], BF16), jax.ShapeDtypeStruct(keep.shape[1:], F32)]
    return whole_call(pair_sum_kernel, "pair_sum", shapes, [], 0, order, keep, got)


def first_sum_kernel(place_ref, keep_ref, got_ref, send_ref):
    for k in range(2):
        total = keep_ref[2 * k + 1].astype(F32) + got_ref[k].astype(F32)
        send_ref[k] = total.astype(BF16)


def first_sum(order, keep, got):
    pair = jax.ShapeDtypeStruct((2, *keep.shape[1:]), BF16)
    return whole_call(first_sum_kernel, "first_sum", [pair], [], 0, order, keep, got)[0]


def last_sum_kernel(place_ref, keep_ref, near_ref, far_ref, send_ref, own_ref):
    for k, out in enumerate((own_ref, send_ref)):
        total = keep_ref[2 * k].astype(F32) + near_ref[k].astype(F32) + far_ref[k].astype(F32)
        out[...] = total.astype(out.dtype)


def last_sum(order, keep, near, far):
    shape = keep.shape[1:]
    shapes = [jax.ShapeDtypeStruct(shape, BF16), jax.ShapeDtypeStruct(shape, F32)]
    return whole_call(last_sum_kernel, "last_sum", shapes, [], 0, order, keep, near, far)


FAR_FIRST = (4, 2, 1)
NEAR_FIRST = (1, 4, 2)


def in_slots(parts, steps=FAR_FIRST):
    first, second, third = steps
    for bits, pair in zip((0, second, third, second ^ third), parts):
        yield bits, pair.at[0]
        yield bits ^ first, pair.at[1]


def lay_rows_kernel(place_ref, *refs):
    *parts, out_ref = refs
    rows = parts[0].shape[-2]
    for j, part in in_slots(parts) if len(parts[0].shape) == 3 else enumerate(parts):
        at = pl.multiple_of((place_ref[0] ^ j) * rows, 8)
        out_ref[pl.ds(at, rows), :] = part[...].astype(F32)


def lay_rows(order, parts):
    rows, columns = parts[0].shape[-2:]
    shape = jax.ShapeDtypeStruct((8 * rows, columns), F32)
    return whole_call(lay_rows_kernel, "lay_rows", [shape], [], 0, order, *parts)[0]


def lay_down_kernel(place_ref, *refs):
    *parts, down_ref, out_ref, vector_ref, full_ref = refs
    slots = list(enumerate(parts)) if len(parts[0].shape) == 2 else list(in_slots(parts))
    rows = parts[0].shape[-2]
    for j, part in slots:
        at = pl.multiple_of((place_ref[0] ^ j) * rows, 8)
        full_ref[pl.ds(at, rows), :] = part[...].astype(F32)
    at = 0
    for out in (down_ref, out_ref, vector_ref):
        out[...] = full_ref[pl.ds(at, out.shape[0]), :]
        at += out.shape[0]


def lay_down(order, parts, units, shard):
    rows, width = parts[0].shape[-2:]
    shapes = [jax.ShapeDtypeStruct((count, width), F32) for count in (units, shard, 8)]
    scratch = [pltpu.VMEM((8 * rows, width), F32)]
    return whole_call(lay_down_kernel, "lay_down", shapes, scratch, 0, order, *parts)


def lay_qkv_kernel(n_parts, place_ref, gain_ref, shift_ref, weight_ref, own_ref, *refs):
    parts, refs = refs[:n_parts], refs[n_parts:]
    out_ref, one_ref, sum_ref, square_ref, row_ref, both_ref, turn_ref = refs
    rows, width = out_ref.shape[0], row_ref.shape[1]
    product, shifted = 0.0, 0.0
    lane = lax.broadcasted_iota(jnp.int32, (1, width), 1)
    counted = (lane % LANES == 0) & (lane < width // LANES * LANES)
    for kind in range(3):
        for j, part in in_slots(parts, NEAR_FIRST):
            at = pl.multiple_of((place_ref[0] ^ j) * LANES, LANES)
            row_ref[:, pl.ds(at, LANES)] = part[:, pl.ds(kind * LANES, LANES)].astype(F32)
        shared = own_ref[:, pl.ds(kind * LANES, LANES)].astype(F32)
        row_ref[:, pl.ds(width - HD, HD)] = shared[:, :HD]
        grad, sums = row_ref[pl.ds(0, rows), :], row_ref[pl.ds(rows, 8), :]
        out_ref[:, pl.ds(kind * width, width)] = grad
        if kind != 1:
            sum_ref[pl.ds(kind // 2, 1), :] = sums[:1]
        total = jnp.sum(jnp.where(counted, sums[1:2], 0.0), axis=1, keepdims=True)
        square_ref[pl.ds(kind, 1), :] = jnp.broadcast_to(total, (1, LANES))
        weight = weight_ref[:, pl.ds(kind * width, width)].astype(F32)
        both_ref[...] = weight * grad
        product = product + jnp.sum(both_ref[...], axis=1, keepdims=True)
        shifted = shifted + jnp.sum(weight * sums[:1], axis=1, keepdims=True)
    for k, column in enumerate((product, shifted)):
        turn_ref[k, pl.ds(0, rows), :] = jnp.broadcast_to(column, (rows, LANES))
    product, shifted = [turn_ref[k].T[:1, :rows] for k in range(2)]
    one_ref[pl.ds(0, 1), :] = (product - shift_ref[...] * shifted) / gain_ref[...]
    one_ref[pl.ds(1, 1), :] = shifted


def lay_qkv(order, gain, shift, weight, own, parts):
    rows, columns = weight.shape
    width = columns // 3
    shapes = [
        jax.ShapeDtypeStruct((rows, columns), F32),
        jax.ShapeDtypeStruct((2, rows), F32),
        jax.ShapeDtypeStruct((2, width), F32),
        jax.ShapeDtypeStruct((3, LANES), F32),
    ]
    scratch = [
        pltpu.VMEM((own.shape[0], width), F32),
        pltpu.VMEM((rows, width), F32),
        pltpu.VMEM((2, -(-rows // LANES) * LANES, LANES), F32),
    ]
    return whole_call(
        functools.partial(lay_qkv_kernel, len(parts)),
        "lay_qkv",
        shapes,
        scratch,
        0,
        order,
        gain,
        shift,
        weight,
        own,
        *parts,
    )


def gather_wsh(block, *others):
    across = swap(block, "wsh", 2)
    if others:
        across = after(across, *others)
    return [block, swap(block, "wsh", 1), across, swap(across, "wsh", 1)]


def scatter_wsh(own, across, send):
    got = swap(send, "wsh", 1)
    return own, got, swap((across + got[1].astype(F32)).astype(BF16), "wsh", 2)


def gather_ctx(block):
    fourth = swap(block, "ctx", 4)
    far = [block, swap(block, "ctx", 2), fourth, swap(fourth, "ctx", 2)]
    near = [swap(part, "ctx", 1) for part in far]
    return [part for pair in zip(far, near) for part in pair]


def gather_pairs(block, steps):
    first, second, third = steps
    pair = jnp.stack([block, swap(block, "ctx", first)])
    across = swap(pair, "ctx", second)
    return [pair, across, swap(pair, "ctx", third), swap(across, "ctx", third)]


def exchange(block):
    return lax.all_to_all(block, "ctx", 0, 0, tiled=True)


def ordered(parts, mine):
    return [
        sum(jnp.where(mine ^ k == i, part, jnp.zeros_like(part)) for k, part in enumerate(parts))
        for i in range(len(parts))
    ]


def by_heads(
    block_in,
    doc_flags,
    ln1_gain,
    ln1_bias,
    w_qkv,
    qv_bias,
    w_out,
    out_bias,
    ln2_gain,
    ln2_bias,
    w_up,
    up_bias,
    w_down,
    down_bias,
    cotangent,
):
    n_ctx, n_wsh = lax.axis_size("ctx"), lax.axis_size("wsh")
    ctx, wsh = lax.axis_index("ctx"), lax.axis_index("wsh")
    place = jnp.stack([ctx, wsh]).astype(jnp.int32)
    tok_rows, width = block_in.shape[1:]
    length = n_ctx * tok_rows
    shard = ln1_gain.shape[0]
    rows_in, rows_grad = block_in[0], cotangent[0]

    order = Order(place)

    blocks = gather_ctx(rows_in)
    packed = (ln1_gain, ln1_bias, qv_bias[:shard], qv_bias[shard:])
    packed += (out_bias, ln2_gain, ln2_bias, down_bias)
    at_row = lax.broadcasted_iota(jnp.int32, (VECTORS, shard), 0)
    packed = sum(jnp.where(at_row == i, vector[None, :], 0) for i, vector in enumerate(packed))
    order.wait(blocks[1])
    weight_parts = gather_wsh(take_columns(order, w_qkv, packed.astype(BF16)))
    vectors = [part[shard : shard + VECTORS, :shard].astype(F32) for part in weight_parts]
    vectors = jnp.concatenate(ordered(vectors, wsh), axis=1)

    qv_full = vectors[2:4].reshape(2, n_wsh, shard).transpose(1, 0, 2).reshape(1, 2 * width)
    gap = jnp.zeros((1, LANES - HD), F32)
    head_shift = jnp.concatenate(
        [
            lax.dynamic_slice_in_dim(qv_full, ctx * LANES, LANES, 1),
            qv_full[:, width - HD : width],
            gap,
            jnp.zeros((1, 2 * LANES), F32),
            lax.dynamic_slice_in_dim(qv_full, width + ctx * LANES, LANES, 1),
            qv_full[:, 2 * width - HD :],
            gap,
        ],
        axis=1,
    )

    flags = after(jnp.broadcast_to(doc_flags, (n_ctx, tok_rows)), blocks[3])
    flags = exchange(flags).reshape(length)
    places = jnp.arange(length, dtype=jnp.int32)
    started = jnp.where(flags == 1, places, 0)
    start_row = jnp.max(
        jnp.where(places[:, None] <= places[None, :], started[:, None], 0), axis=0, keepdims=True
    )

    normed_one, qkv, attended, log_total, own_low, low = attend_forward(
        order, start_row, vectors, head_shift, blocks, weight_parts
    )
    grads = gather_wsh(after(rows_grad, weight_parts[2]), low)
    out_parts = gather_wsh(after(w_out, weight_parts[3]), low)
    parts = exchange(low)
    act_grad_near, act_grad_far = act_back(order, grads, w_down)
    *lows, residual, normed_two, branch_square = out_project(
        order, own_low, rows_in, vectors, parts, out_parts
    )
    unit_shift = up_bias.astype(F32).reshape(1, -1)
    two_near = swap(normed_two, "wsh", 1)
    two_across = swap(normed_two, "wsh", 2)
    act_near, pre_near, back_0, back_1, up_sum_near = feed(
        order, normed_two, two_near, act_grad_near, w_up, unit_shift, "feed_near"
    )
    two_across = after(two_across, back_1)
    two_far = swap(two_across, "wsh", 1)
    act_far, pre_far, back_2, back_3, up_sum_far = feed(
        order, two_across, two_far, act_grad_far, w_up, unit_shift, "feed_far"
    )

    back_near = swap(back_1, "wsh", 1)
    back_across = swap((back_2 + swap(back_3, "wsh", 1).astype(F32)).astype(BF16), "wsh", 2)
    lows = [lows[0]] + [swap(after(lows[k], back_1), "wsh", k) for k in (1, 2, 3)]
    send, keep_up = grad_halves(
        order, [normed_two, two_near, two_across, two_far], [pre_near, pre_far], "grad_up"
    )
    got_up = swap(send, "ctx", 1)
    residual_grad, attn_grad, head_grad = residual_back(
        order, back_0, back_near, back_across, residual, rows_grad, vectors, out_parts, n_ctx
    )
    attn_parts = gather_wsh(attn_grad)
    grad_parts = exchange(head_grad)
    outs = scatter_wsh(*feed_out(order, act_near, act_far, w_down))
    down_first, down_second, keep_down = down_halves(
        order, up_sum_near, up_sum_far, [act_near, act_far], grads, lows, attn_parts, True
    )
    down_first, down_second = swap(down_first, "ctx", 1), swap(down_second, "ctx", 1)
    send, keep_up = half_sum(order, keep_up, got_up)
    far_up = swap(send, "ctx", 2)
    qkv_grad, own_grad, qkv_send = attend_backward(
        order, start_row, qkv, attended, log_total, grad_parts, tok_rows
    )
    qkv_parts = exchange(qkv_send)
    send, own_up = pair_sum(order, keep_up, far_up)
    up_piece = (own_up + swap(send, "ctx", 4).astype(F32)).astype(BF16)
    up_parts = gather_pairs(up_piece, FAR_FIRST)
    quarters = scatter_wsh(*grad_qkv_quarters(order, normed_one, qkv_grad))
    down_far = swap(first_sum(order, keep_down, down_first), "ctx", 2)
    send, own_down = last_sum(order, keep_down, down_second, down_far)
    down_piece = (own_down + swap(send, "ctx", 4).astype(F32)).astype(BF16)
    down_parts = gather_ctx(down_piece)
    order.wait(qkv_parts)
    block_out, squares = block_sum(order, residual, *outs, vectors)
    pair_piece, own_piece = qkv_piece(order, *quarters, branch_square, squares)
    pair_parts = gather_pairs(pair_piece, NEAR_FIRST)
    weight_full = gather_wsh(after(w_qkv, own_up))
    input_grad = input_back(
        order, own_grad, rows_in, residual_grad, vectors, qkv_parts, weight_full
    )
    grad_up = lay_rows(order, up_parts)
    gain_row, shift_row = [v.astype(F32).reshape(1, shard) for v in (ln1_gain, ln1_bias)]
    grad_qkv, sum_one, sum_qv, squares = lay_qkv(
        order, gain_row, shift_row, w_qkv, own_piece, pair_parts
    )
    grad_down, grad_out, sums = lay_down(order, down_parts, w_down.shape[0], shard)
    rms_values = jnp.sqrt(squares[:, 0] / (length * width)).reshape(1, 3)
    mine = lax.dynamic_slice_in_dim(sums[:4], wsh * shard, shard, 1)

    return (
        block_out[None],
        input_grad[None],
        sum_one[0],
        sum_one[1],
        grad_qkv,
        lax.dynamic_slice_in_dim(sum_qv.reshape(2 * width), wsh * 2 * shard, 2 * shard),
        grad_out,
        mine[1],
        mine[2],
        mine[3],
        grad_up,
        sums[4],
        grad_down,
        mine[0],
        rms_values,
    )


def prefix(shard, axis, combine, identity):
    size, mine = (lax.axis_size(axis), lax.axis_index(axis))
    everything = lax.all_gather(shard, axis)
    start = jnp.broadcast_to(jnp.asarray(identity, shard.dtype), shard.shape)

    def step(k, before):
        reached = k < mine
        new = combine(before, everything[k])
        return jnp.where(reached, new, before)

    return lax.fori_loop(0, size, step, start)


def normed(values, gain, shift):
    centre = values - jnp.mean(values, axis=-1, keepdims=True)
    spread = jnp.mean(centre * centre, axis=-1, keepdims=True)
    return centre * lax.rsqrt(spread + EPSILON) * gain + shift


def gelu_tanh(values):
    return jax.nn.gelu(values, approximate=True)


def add_counts(earlier, later):
    return earlier + later


def allowed_pairs(query_segment, query_place, key_segment, key_place):
    return (
        (query_segment[:, None] == key_segment[None, :])
        & (key_place[None, :] <= query_place[:, None])
    )[:, None, :]


def score_pairs(query_rows, key_rows, scaling):
    return (
        jnp.einsum("qhd,khd->qhk", query_rows, key_rows, preferred_element_type=jnp.float32)
        * scaling
    )


def contract_rows(left, right):
    return lax.dot_general(
        left, right, (((0,), (0,)), ((), ())), preferred_element_type=jnp.float32
    )


def contract_cols(left, right):
    return lax.dot_general(
        left, right, (((1,), (1,)), ((), ())), preferred_element_type=jnp.float32
    )


def by_tokens(
    block_in,
    doc_flags,
    ln1_gain,
    ln1_bias,
    w_qkv,
    qv_bias,
    w_out,
    out_bias,
    ln2_gain,
    ln2_bias,
    w_up,
    up_bias,
    w_down,
    down_bias,
    cotangent,
):
    tok_rows = block_in.shape[1]
    model_width = block_in.shape[2]
    scaling = HD ** (-0.5)
    ctx_count = lax.axis_size("ctx")
    earlier = jnp.arange(tok_rows)
    running_count = jnp.sum(
        jnp.where(earlier[None, :] <= earlier[:, None], doc_flags[0][None, :], 0), axis=1
    )
    offset_count = prefix(running_count[-1], "ctx", add_counts, jnp.int32(0))
    local_segment = running_count + offset_count - 1
    local_place = lax.axis_index("ctx") * tok_rows + jnp.arange(tok_rows, dtype=jnp.int32)
    (
        gain_one,
        shift_one,
        qkv_full,
        qv_full,
        out_full,
        out_shift,
        gain_two,
        shift_two,
        up_full,
        up_shift,
        down_full,
        down_shift,
    ) = (
        lax.all_gather(ln1_gain, "wsh", axis=0, tiled=True),
        lax.all_gather(ln1_bias, "wsh", axis=0, tiled=True),
        lax.all_gather(w_qkv, "wsh", axis=0, tiled=True),
        lax.all_gather(qv_bias, "wsh", axis=0, tiled=True),
        lax.all_gather(w_out, "wsh", axis=0, tiled=True),
        lax.all_gather(out_bias, "wsh", axis=0, tiled=True),
        lax.all_gather(ln2_gain, "wsh", axis=0, tiled=True),
        lax.all_gather(ln2_bias, "wsh", axis=0, tiled=True),
        lax.all_gather(w_up, "wsh", axis=1, tiled=True),
        lax.all_gather(up_bias, "wsh", axis=0, tiled=True),
        lax.all_gather(w_down, "wsh", axis=0, tiled=True),
        lax.all_gather(down_bias, "wsh", axis=0, tiled=True),
    )
    gain_one, shift_one, gain_two, shift_two = [
        vector.astype(jnp.float32) for vector in (gain_one, shift_one, gain_two, shift_two)
    ]
    out_shift, up_shift, down_shift = [
        vector.astype(jnp.float32) for vector in (out_shift, up_shift, down_shift)
    ]
    input_rows = block_in[0].astype(jnp.float32)
    normed_one = normed(input_rows, gain_one, shift_one).astype(jnp.bfloat16)
    qkv_shift = jnp.concatenate(
        [qv_full[:model_width], jnp.zeros((model_width,), qv_full.dtype), qv_full[model_width:]]
    ).astype(jnp.float32)
    projected = (
        jnp.dot(normed_one, qkv_full, preferred_element_type=jnp.float32) + qkv_shift
    ).astype(jnp.bfloat16)
    queries = projected[:, :model_width].reshape(tok_rows, H, HD)
    key_rows = projected[:, model_width : 2 * model_width].reshape(tok_rows, H, HD)
    value_rows = projected[:, 2 * model_width :].reshape(tok_rows, H, HD)
    key_piece = lax.all_gather(key_rows, "ctx", axis=0, tiled=True)
    value_piece = lax.all_gather(value_rows, "ctx", axis=0, tiled=True)
    segment_piece = lax.all_gather(local_segment, "ctx", axis=0, tiled=True)
    piece_place = jnp.arange(key_piece.shape[0], dtype=jnp.int32)
    row_best = jnp.full((tok_rows, H), NEGATIVE, jnp.float32)
    score_block = score_pairs(queries, key_piece, scaling)
    allowed = allowed_pairs(local_segment, local_place, segment_piece, piece_place)
    new_best = jnp.maximum(row_best, jnp.max(jnp.where(allowed, score_block, NEGATIVE), axis=-1))
    weight_block = jnp.where(allowed, jnp.exp(score_block - new_best[..., None]), 0.0)
    row_total = jnp.sum(weight_block, axis=-1)
    weighted = jnp.einsum(
        "qhk,khd->qhd",
        weight_block.astype(jnp.bfloat16),
        value_piece,
        preferred_element_type=jnp.float32,
    )
    row_best, row_total, weighted = (new_best, row_total, weighted)
    log_total = row_best + jnp.log(row_total)
    attended = weighted / row_total[..., None]
    attended_low = attended.reshape(tok_rows, model_width).astype(jnp.bfloat16)
    attn_branch = jnp.dot(attended_low, out_full, preferred_element_type=jnp.float32) + out_shift
    residual = input_rows + attn_branch
    normed_two = normed(residual, gain_two, shift_two).astype(jnp.bfloat16)
    hidden_pre = jnp.dot(normed_two, up_full, preferred_element_type=jnp.float32) + up_shift
    hidden_act = gelu_tanh(hidden_pre).astype(jnp.bfloat16)
    mlp_sum = jnp.dot(hidden_act, down_full, preferred_element_type=jnp.float32)
    mlp_branch = mlp_sum + down_shift
    block_full = residual + mlp_branch
    square_sums = lax.psum(
        jnp.stack(
            [
                jnp.sum(attn_branch * attn_branch),
                jnp.sum(mlp_branch * mlp_branch),
                jnp.sum(block_full * block_full),
            ]
        ),
        "ctx",
    )
    rms_values = jnp.sqrt(square_sums / (tok_rows * ctx_count * model_width)).reshape(1, 3)
    out_grad = cotangent[0].astype(jnp.float32)
    mlp_grad = out_grad.astype(jnp.bfloat16)
    grad_down_shift = jnp.sum(mlp_grad.astype(jnp.float32), axis=0)
    grad_down = contract_rows(hidden_act, mlp_grad)
    act_grad = contract_cols(mlp_grad, down_full)
    unused_act, gelu_pull = jax.vjp(gelu_tanh, hidden_pre)
    pre_grad = gelu_pull(act_grad)[0].astype(jnp.bfloat16)
    grad_up_shift = jnp.sum(pre_grad.astype(jnp.float32), axis=0)
    grad_up = contract_rows(normed_two, pre_grad)
    normed_two_grad = contract_cols(pre_grad, up_full)
    unused_two, norm_two_pull = jax.vjp(normed, residual, gain_two, shift_two)
    residual_ln, grad_gain_two, grad_shift_two = norm_two_pull(normed_two_grad)
    residual_grad = out_grad + residual_ln
    attn_grad = residual_grad.astype(jnp.bfloat16)
    grad_out_shift = jnp.sum(attn_grad.astype(jnp.float32), axis=0)
    grad_out = contract_rows(attended_low, attn_grad)
    attended_grad = contract_cols(attn_grad, out_full).astype(jnp.bfloat16).reshape(tok_rows, H, HD)
    row_delta = jnp.sum(attended_grad.astype(jnp.float32) * attended, axis=-1)
    key_piece = lax.all_gather(key_rows, "ctx", axis=0, tiled=True)
    value_piece = lax.all_gather(value_rows, "ctx", axis=0, tiled=True)
    segment_piece = lax.all_gather(local_segment, "ctx", axis=0, tiled=True)
    piece_place = jnp.arange(key_piece.shape[0], dtype=jnp.int32)
    score_block = score_pairs(queries, key_piece, scaling)
    allowed = allowed_pairs(local_segment, local_place, segment_piece, piece_place)
    probability = jnp.where(allowed, jnp.exp(score_block - log_total[..., None]), 0.0)
    prob_grad = jnp.einsum(
        "qhd,khd->qhk", attended_grad, value_piece, preferred_element_type=jnp.float32
    )
    score_grad = (probability * (prob_grad - row_delta[..., None])).astype(jnp.bfloat16)
    query_grad = scaling * jnp.einsum(
        "qhk,khd->qhd", score_grad, key_piece, preferred_element_type=jnp.float32
    )
    query_piece = lax.all_gather(
        queries.astype(jnp.float32).astype(jnp.bfloat16), "ctx", axis=0, tiled=True
    ).astype(jnp.float32)
    grad_piece = lax.all_gather(
        attended_grad.astype(jnp.float32).astype(jnp.bfloat16), "ctx", axis=0, tiled=True
    )
    total_piece = lax.all_gather(log_total.astype(jnp.bfloat16), "ctx", axis=0, tiled=True).astype(
        jnp.float32
    )
    delta_piece = lax.all_gather(row_delta.astype(jnp.bfloat16), "ctx", axis=0, tiled=True).astype(
        jnp.float32
    )
    segment_piece = lax.all_gather(local_segment, "ctx", axis=0, tiled=True)
    query_low = query_piece.astype(jnp.bfloat16)
    piece_place = jnp.arange(query_piece.shape[0], dtype=jnp.int32)
    score_block = score_pairs(query_low, key_rows, scaling)
    allowed = allowed_pairs(segment_piece, piece_place, local_segment, local_place)
    probability = jnp.where(allowed, jnp.exp(score_block - total_piece[..., None]), 0.0)
    value_grad = jnp.einsum(
        "qhk,qhd->khd",
        probability.astype(jnp.bfloat16),
        grad_piece,
        preferred_element_type=jnp.float32,
    )
    prob_grad = jnp.einsum(
        "qhd,khd->qhk", grad_piece, value_rows, preferred_element_type=jnp.float32
    )
    score_grad = (probability * (prob_grad - delta_piece[..., None])).astype(jnp.bfloat16)
    key_grad = scaling * jnp.einsum(
        "qhk,qhd->khd", score_grad, query_low, preferred_element_type=jnp.float32
    )
    key_grad, value_grad = (key_grad, value_grad)
    qkv_grad = jnp.concatenate(
        [
            query_grad.reshape(tok_rows, model_width),
            key_grad.reshape(tok_rows, model_width),
            value_grad.reshape(tok_rows, model_width),
        ],
        axis=1,
    ).astype(jnp.bfloat16)
    qkv_grad_wide = qkv_grad.astype(jnp.float32)
    grad_qv_shift = jnp.concatenate(
        [
            jnp.sum(qkv_grad_wide[:, :model_width], axis=0),
            jnp.sum(qkv_grad_wide[:, 2 * model_width :], axis=0),
        ]
    )
    grad_qkv = contract_rows(normed_one, qkv_grad)
    normed_one_grad = contract_cols(qkv_grad, qkv_full)
    unused_one, norm_one_pull = jax.vjp(normed, input_rows, gain_one, shift_one)
    input_ln, grad_gain_one, grad_shift_one = norm_one_pull(normed_one_grad)
    input_grad = (residual_grad + input_ln).astype(jnp.bfloat16)
    (
        sum_gain_one,
        sum_shift_one,
        sum_qkv,
        sum_qv_shift,
        sum_out,
        sum_out_shift,
        sum_gain_two,
        sum_shift_two,
        sum_up,
        sum_up_shift,
        sum_down,
        sum_down_shift,
    ) = (
        lax.psum_scatter(
            grad_gain_one.astype(jnp.bfloat16), "wsh", scatter_dimension=0, tiled=True
        ).astype(jnp.float32),
        lax.psum_scatter(
            grad_shift_one.astype(jnp.bfloat16), "wsh", scatter_dimension=0, tiled=True
        ).astype(jnp.float32),
        lax.psum_scatter(
            grad_qkv.astype(jnp.bfloat16), "wsh", scatter_dimension=0, tiled=True
        ).astype(jnp.float32),
        lax.psum_scatter(
            grad_qv_shift.astype(jnp.bfloat16), "wsh", scatter_dimension=0, tiled=True
        ).astype(jnp.float32),
        lax.psum_scatter(
            grad_out.astype(jnp.bfloat16), "wsh", scatter_dimension=0, tiled=True
        ).astype(jnp.float32),
        lax.psum_scatter(
            grad_out_shift.astype(jnp.bfloat16), "wsh", scatter_dimension=0, tiled=True
        ).astype(jnp.float32),
        lax.psum_scatter(
            grad_gain_two.astype(jnp.bfloat16), "wsh", scatter_dimension=0, tiled=True
        ).astype(jnp.float32),
        lax.psum_scatter(
            grad_shift_two.astype(jnp.bfloat16), "wsh", scatter_dimension=0, tiled=True
        ).astype(jnp.float32),
        lax.psum_scatter(
            grad_up.astype(jnp.bfloat16), "wsh", scatter_dimension=1, tiled=True
        ).astype(jnp.float32),
        lax.psum_scatter(
            grad_up_shift.astype(jnp.bfloat16), "wsh", scatter_dimension=0, tiled=True
        ).astype(jnp.float32),
        lax.psum_scatter(
            grad_down.astype(jnp.bfloat16), "wsh", scatter_dimension=0, tiled=True
        ).astype(jnp.float32),
        lax.psum_scatter(
            grad_down_shift.astype(jnp.bfloat16), "wsh", scatter_dimension=0, tiled=True
        ).astype(jnp.float32),
    )
    totals = lax.psum(
        (
            sum_gain_one,
            sum_shift_one,
            sum_qkv,
            sum_qv_shift,
            sum_out,
            sum_out_shift,
            sum_gain_two,
            sum_shift_two,
            sum_up,
            sum_up_shift,
            sum_down,
            sum_down_shift,
        ),
        "ctx",
    )
    return (
        block_full.astype(jnp.bfloat16)[None],
        input_grad[None],
        totals[0],
        totals[1],
        totals[2],
        totals[3],
        totals[4],
        totals[5],
        totals[6],
        totals[7],
        totals[8],
        totals[9],
        totals[10],
        totals[11],
        rms_values,
    )


def solution(mesh):
    each = LANES // HD
    by_head = mesh.shape["ctx"] == 8 and mesh.shape["ctx"] * each + 1 == H and mesh.shape["wsh"] == 4
    return jax.shard_map(
        by_heads if by_head else by_tokens,
        mesh=mesh,
        in_specs=(
            P("wsh", "ctx", None),
            P("wsh", "ctx"),
            P("wsh"),
            P("wsh"),
            P("wsh", None),
            P("wsh"),
            P("wsh", None),
            P("wsh"),
            P("wsh"),
            P("wsh"),
            P(None, "wsh"),
            P("wsh"),
            P("wsh", None),
            P("wsh"),
            P("wsh", "ctx", None),
        ),
        out_specs=(
            P("wsh", "ctx", None),
            P("wsh", "ctx", None),
            P("wsh"),
            P("wsh"),
            P("wsh", None),
            P("wsh"),
            P("wsh", None),
            P("wsh"),
            P("wsh"),
            P("wsh"),
            P(None, "wsh"),
            P("wsh"),
            P("wsh", None),
            P("wsh"),
            P("wsh", None),
        ),
        check_vma=False,
    )
```
